512 devices in a mesh: dom: 32 (over z, y_lo), sp: 16 (over x, y_hi, core).
Axes of the slice: x: 4, y: 4 (y_hi: 2, y_lo: 2; y = y_hi * 2 + y_lo), z: 16, core: 2. Of those that a mesh axis runs over, the one named last changes fastest.
Arguments:
- descriptors: bfloat16 [4096, 2048], P('dom', 'sp'), may hold values from -6 to 6
- sparse_points: bfloat16 [32768, 2048], P('sp', 'dom'), may hold values from -6 to 6
- coefficients: float32 [32768], P('sp'), may hold values from -0.0078125 to 0.0078125
- derivatives: bfloat16 [4096, 3, 12, 2048], P('dom', None, None, 'sp'), may hold values from -4 to 4
- neighbours: int32 [4096, 12], P('dom'), may hold values from 0 to 383
- counts: int32 [4096], P('dom'), may hold values from 3 to 12, as said below
- ghost_index: int32 [8192], P('dom'), may hold values from 0 to 127
Outputs:
- forces: float32 [3, 4096], P(None, 'dom')
- energies: float32 [4096], P('dom')
The draws below stay inside these ranges and needn't reach their ends.
Inputs may be any that keep to these rules, and one draw needn't show every extreme that they name: `counts`: each atom has between 3 and 12 live neighbour slots; the first atom of every domain has all 12.
All inputs are finite; a program needn't handle non-finite values.
Results may differ from the reference program's by a relative error of at most 0.0056.
Values may be sent and summed in bfloat16 or wider, within the bound.
No kernel may reach another device: no remote copies, remote signals or barrier semaphores. Data moves between devices by JAX's collectives and lax.ppermute only.
A program may use at most 64 MiB of HBM per device.

```python
import jax
import jax.numpy as jnp
from jax import lax

D = 2048
A_DEV = 128
NBR = 12
GHOST = 128
ATOMS = 4096
M = 32768
N_DOM = 32


def draw_counts(key, part):
    key = jax.random.fold_in(key, 7)
    base = jax.random.randint(key, (ATOMS,), NBR // 4, NBR + 1)
    first = jnp.arange(ATOMS, dtype=jnp.int32) % A_DEV == 0
    return jnp.where(first, NBR, base).astype(jnp.int32)


def plant(array, key, low, high):
    longest = array.shape.index(max(array.shape))
    spots = []
    for shift in (0, 1):
        where = [jax.random.randint(jax.random.fold_in(key, axis), (), 0, length) for axis, length in enumerate(array.shape)]
        where[longest] = (where[longest] + shift) % array.shape[longest]
        spots.append(tuple(where))
    return array.at[spots[0]].set(low).at[spots[1]].set(high)


def steps_of(stream_key, extent, cuts, low, largest):
    loudness, own = 1.0, jax.random.fold_in(stream_key, 6)
    for dim, blocks in cuts:
        draws = jnp.exp(jax.random.uniform(jax.random.fold_in(own, dim), (blocks,), jnp.float32, low / len(cuts), largest / len(cuts)))
        loudness = loudness * jnp.repeat(draws, extent[dim] // blocks).reshape([-1 if axis == dim else 1 for axis in range(len(extent))])
    return loudness


def centred(rng, dims, scale, most, pieces=(), kind=jnp.bfloat16):
    gain = steps_of(rng, dims, pieces, -0.22, 0.18) if pieces else 1.0
    drawn = jax.random.normal(rng, dims, jnp.float32) * scale * gain
    return jnp.minimum(jnp.maximum(drawn, -most), most).astype(kind)


def setup_inputs(seed: int = 0) -> dict:
    keys = jax.random.split(jax.random.key(seed), 8)
    descriptors = centred(keys[0], (ATOMS, D), 1.0, 6.0, ((0, 32), (1, 16)))
    sparse_points = centred(keys[1], (M, D), 1.0, 6.0, ((0, 16), (1, 32)))
    coefficients = centred(keys[2], (M,), 0.0005, 0.0078125, ((0, 16),), jnp.float32)
    derivatives = centred(keys[3], (ATOMS, 3, NBR, D), 0.3, 4.0, ((0, 32), (3, 16)))
    neighbours = plant(jax.random.randint(keys[4], (ATOMS, NBR), 0, A_DEV + 2 * GHOST), jax.random.fold_in(keys[4], 1), 0, (A_DEV + 2 * GHOST) - 1).astype(jnp.int32)
    counts = draw_counts(jax.random.fold_in(keys[7], 71), 0)
    ghost_index = plant(jax.random.randint(keys[6], (N_DOM * 2 * GHOST,), 0, A_DEV), jax.random.fold_in(keys[6], 1), 0, A_DEV - 1).astype(jnp.int32)
    return {"descriptors": descriptors, "sparse_points": sparse_points, "coefficients": coefficients, "derivatives": derivatives, "neighbours": neighbours, "counts": counts, "ghost_index": ghost_index}


def domain_terms(sparse_points, coefficients, descriptors, derivatives, neighbours, counts):
    values = descriptors.astype(jnp.float32)
    row_norm = jnp.sqrt(lax.optimization_barrier(jnp.sum(values * values, axis=1, keepdims=True)) + 1e-06)
    unit_rows = (values / row_norm).astype(jnp.bfloat16)
    kernel = lax.dot_general(unit_rows, sparse_points, (((1,), (1,)), ((), ())), preferred_element_type=jnp.float32)
    energies = lax.optimization_barrier(jnp.sum(coefficients[None, :] * kernel ** 4, axis=1))
    slopes = (4.0 * coefficients[None, :] * kernel ** 3).astype(jnp.bfloat16)
    gradient = jnp.dot(slopes, sparse_points, preferred_element_type=jnp.float32)
    unit_float = unit_rows.astype(jnp.float32)
    inner = lax.optimization_barrier(jnp.sum(unit_float * gradient, axis=1, keepdims=True))
    descent = ((gradient - unit_float * inner) / row_norm).astype(jnp.bfloat16)
    partial_value = jnp.einsum('ad,acnd->acn', descent.astype(jnp.float32), derivatives.astype(jnp.float32))
    live = jnp.arange(NBR, dtype=jnp.int32)[None, :] < counts[:, None]
    partial_value = jnp.where(live[:, None, :], partial_value, jnp.float32(0.0))
    moved = jnp.transpose(partial_value, (1, 0, 2))
    extended = jnp.zeros((3, A_DEV + 2 * GHOST), jnp.float32).at[:, neighbours].add(-moved)
    extended = extended.at[:, :A_DEV].add(lax.optimization_barrier(jnp.sum(moved, axis=2)))
    return (energies, extended)

def reference(descriptors, sparse_points, coefficients, derivatives, neighbours, counts, ghost_index):

    def per_domain(items):
        return domain_terms(sparse_points, coefficients, items[0], items[1], items[2], items[3])
    energies, extended = lax.map(per_domain, (descriptors.reshape(N_DOM, A_DEV, D), derivatives.reshape(N_DOM, A_DEV, 3, NBR, D), neighbours.reshape(N_DOM, A_DEV, NBR), counts.reshape(N_DOM, A_DEV)))
    owners = ghost_index.reshape(N_DOM, 2, GHOST)

    def return_side(amounts, index):
        return jnp.zeros((3, A_DEV), jnp.float32).at[:, index].add(amounts)
    to_left = jax.vmap(return_side)(extended[:, :, A_DEV:A_DEV + GHOST], owners[:, 0])
    to_right = jax.vmap(return_side)(extended[:, :, A_DEV + GHOST:], owners[:, 1])
    total = extended[:, :, :A_DEV] + jnp.roll(to_left, -1, axis=0) + jnp.roll(to_right, 1, axis=0)
    forces = jnp.transpose(total, (1, 0, 2)).reshape(3, ATOMS)
    return (forces, energies.reshape(ATOMS))
```

```python
import jax
import jax.numpy as jnp
from jax import lax
from jax.sharding import Mesh, PartitionSpec as P

DOM = ("z", "yl")
SP = ("x", "yh", "c")
PLANE = ("yl", "x", "yh", "c")


def pieces(value):
    high = lax.reduce_precision(value, 8, 7)
    rest = value - high
    mid = lax.reduce_precision(rest, 8, 7)
    return [p.astype(jnp.bfloat16) for p in (high, mid, rest - mid)]


def body(descriptors, sparse_points, coefficients, derivatives, neighbours, counts, ghost_index):
    f32, bf16 = jnp.float32, jnp.bfloat16
    yl = lax.axis_index("yl")
    owned, width = descriptors.shape
    points, part = sparse_points.shape
    n_sp, n_plane = lax.axis_size(SP), lax.axis_size(PLANE)
    half = points // 2
    slots_count = neighbours.shape[1]
    ghosts = ghost_index.shape[0] // 2

    with jax.named_scope("points_swap"):
        split = jnp.transpose(sparse_points.T.reshape(part, 2, half), (1, 0, 2))
        swapped = lax.all_to_all(split, "yl", 0, 0).reshape(2 * part, half)
    with jax.named_scope("points_gather"):
        basis = lax.all_gather(swapped, "z", axis=0, tiled=True)

    with jax.named_scope("descriptors_gather"):
        spread = jnp.broadcast_to(descriptors[None], (n_plane, owned, width))
        blocks = lax.all_to_all(spread, PLANE, 0, 0).reshape(2, n_sp, owned, width)
        rows = jnp.transpose(blocks, (0, 2, 1, 3)).reshape(2 * owned, n_sp * width)
    values = rows.astype(f32)
    row_norm = jnp.sqrt(jnp.sum(values * values, axis=1, keepdims=True) + 1e-06)
    unit_rows = (values / row_norm).astype(bf16)
    own_norm = lax.dynamic_slice_in_dim(row_norm, yl * owned, owned, 0)
    own_unit = (descriptors.astype(f32) / own_norm).astype(bf16).astype(f32)

    with jax.named_scope("scatter_table"):
        slot_total = owned + 2 * ghosts
        flat = neighbours.reshape(owned * slots_count)
        slot_ids = jnp.arange(slot_total, dtype=jnp.int32)
        hot = (flat[:, None] == slot_ids[None, :]).astype(bf16)
        target = jnp.concatenate(
            [
                jnp.arange(owned, dtype=jnp.int32),
                ghost_index[:ghosts] + owned,
                ghost_index[ghosts:] + 2 * owned,
            ]
        )
        column_ids = jnp.arange(3 * owned, dtype=jnp.int32)
        moves = (target[:, None] == column_ids[None, :]).astype(bf16)
        landed = jnp.dot(hot, moves, preferred_element_type=f32)
        atom_of = jnp.arange(owned * slots_count, dtype=jnp.int32) // slots_count
        slot_of = jnp.arange(owned * slots_count, dtype=jnp.int32) % slots_count
        self_hot = (atom_of[:, None] == column_ids[None, :]).astype(f32)
        live = slot_of < jnp.repeat(counts, slots_count)
        table = jnp.where(live[:, None], self_hot - landed, 0.0).astype(bf16)

    with jax.named_scope("kernel"):
        kernel = jnp.dot(unit_rows, basis, preferred_element_type=f32)
        mine = lax.dynamic_slice_in_dim(coefficients, yl * half, half, 0)[None, :]
        cube = mine * kernel**3
        energy_part = jnp.sum(cube * kernel, axis=1)
        slopes = (4.0 * cube).astype(bf16)
        inner_part = jnp.sum(slopes.astype(f32) * kernel, axis=1)
    with jax.named_scope("gradient"):
        gradient = lax.dot_general(
            slopes, basis, (((1,), (1,)), ((), ())), preferred_element_type=f32
        ).astype(bf16)
        shares = jnp.transpose(gradient.reshape(2, owned, n_sp, width), (0, 2, 1, 3))
        extra = jnp.stack(pieces(energy_part) + pieces(inner_part)).reshape(6, 2, owned)
        extra = jnp.pad(jnp.transpose(extra, (1, 0, 2)), ((0, 0), (0, 10), (0, 0)))
        extra = jnp.broadcast_to(extra[:, None], (2, n_sp, 16, owned))
        outgoing = jnp.concatenate([shares, extra], axis=2).reshape(n_plane, owned + 16, width)
    with jax.named_scope("gradient_exchange"):
        total = jnp.sum(lax.all_to_all(outgoing, PLANE, 0, 0).astype(f32), axis=0)
    share = total[:owned]
    energies = total[owned] + total[owned + 1] + total[owned + 2]
    inner = (total[owned + 3] + total[owned + 4] + total[owned + 5])[:, None]
    descent = ((share - own_unit * inner) / own_norm).astype(bf16)
    with jax.named_scope("contract"):
        partial = jnp.einsum("ad,acnd->can", descent, derivatives, preferred_element_type=f32)
    with jax.named_scope("scatter"):
        partial = partial.reshape(3, owned * slots_count)
        moved = jnp.dot(jnp.concatenate(pieces(partial)), table, preferred_element_type=f32)
        moved = moved[0:3] + moved[3:6] + moved[6:9]
        own, to_left, to_right = jnp.split(moved, 3, axis=1)
    with jax.named_scope("ghosts"):
        first = yl == 0
        across = jnp.where(first, to_left, to_right)
        beside = jnp.where(first, to_right, to_left)
        size = lax.axis_size(DOM)
        pairs = [(i, (i - 1) % size if i % 2 == 0 else (i + 1) % size) for i in range(size)]
        own = own + lax.ppermute(across, DOM, pairs)
        both = jnp.stack([jnp.where(first, own, beside), jnp.where(first, beside, own)])
        both = jnp.broadcast_to(both[:, None], (2, n_sp, 3, owned)).reshape(n_plane, 3, owned)
        forces = jnp.sum(lax.all_to_all(both, PLANE, 0, 0), axis=0)
    return (forces, energies)


def solution(mesh):
    grid = Mesh(mesh.devices.reshape(16, 2, 4, 2, 2), ("z", "yl", "x", "yh", "c"))
    return jax.shard_map(
        body,
        mesh=grid,
        in_specs=(
            P(DOM, SP),
            P(SP, DOM),
            P(SP),
            P(DOM, None, None, SP),
            P(DOM, None),
            P(DOM),
            P(DOM),
        ),
        out_specs=(P(None, DOM), P(DOM)),
        check_vma=False,
    )
```

```python
import jax
import jax.numpy as jnp
from jax import lax
from jax.experimental import pallas as pl
from jax.experimental.pallas import tpu as pltpu
from jax.sharding import Mesh, PartitionSpec as P

DOM = ("z", "yl")
SP = ("x", "yh", "c")
CHIPS = ("yl", "x", "yh")
PLANE = ("yl", "x", "yh", "c")
CHUNKS = 4
F32, BF16 = jnp.float32, jnp.bfloat16
LAST = (((1,), (1,)), ((), ()))


def main_kernel(
    core_ref, unit_ref, scale_ref, coef_ref, basis_hbm, own_ref, other_ref, energy_ref,
    basis, kernel, slopes, inner, sems,
):
    columns = basis.shape[0]
    step = columns // CHUNKS
    atoms = unit_ref.shape[0]
    half = atoms // 2
    copies = [
        pltpu.make_async_copy(
            basis_hbm.at[pl.ds(i * step, step)], basis.at[pl.ds(i * step, step)], sems.at[i]
        )
        for i in range(CHUNKS)
    ]
    for copy in copies:
        copy.start()
    for i, copy in enumerate(copies):
        copy.wait()
        term = jnp.dot(
            unit_ref[:, i * step : (i + 1) * step],
            basis[i * step : (i + 1) * step, :],
            preferred_element_type=F32,
        )
        if i == 0:
            kernel[...] = term
        else:
            kernel[...] += term
    four = 4.0 * coef_ref[...]
    block = 32
    for r in range(0, atoms, block):
        k = kernel[r : r + block, :]
        s = four * (k * k * k)
        low = s.astype(BF16)
        slopes[r : r + block, :] = low
        inner[r : r + block, :] = jnp.broadcast_to(
            jnp.sum(low.astype(F32) * k, axis=1, keepdims=True), (block, 128)
        )
        kernel[r : r + block, 0:128] = jnp.broadcast_to(
            0.25 * jnp.sum(s * k, axis=1, keepdims=True), (block, 128)
        )
    for y in range(2):
        energy_ref[y] = kernel[y * half : (y + 1) * half, 0:128].T[0:8, :]
    even_first = core_ref[0] == 0
    for j in range(columns // 256):
        g = lax.dot_general(
            slopes[...], basis[j * 256 : (j + 1) * 256, :], LAST, preferred_element_type=F32
        )
        for p in range(2):
            at = slice(j * 256 + p * 128, j * 256 + (p + 1) * 128)
            u = unit_ref[:, at].astype(F32)
            part = (g[:, p * 128 : (p + 1) * 128] - u * inner[...]) * scale_ref[...]

            @pl.when(even_first if p == 0 else jnp.logical_not(even_first))
            def _():
                own_ref[0, j] = part[:half]
                own_ref[1, j] = part[half:]

            @pl.when(jnp.logical_not(even_first) if p == 0 else even_first)
            def _():
                other_ref[0, j] = part[:half]
                other_ref[1, j] = part[half:]


def tail_kernel(parts_ref, deriv_ref, table_ref, out_ref):
    total = parts_ref[0].astype(F32)
    for i in range(1, parts_ref.shape[0]):
        total += parts_ref[i].astype(F32)
    atoms = total.shape[0]
    pairs = deriv_ref.shape[2]
    high = total.astype(BF16)
    low = (total - high.astype(F32)).astype(BF16)
    both = jnp.concatenate([high, low], axis=0)
    slots = pairs // atoms
    row = lax.broadcasted_iota(jnp.int32, (atoms, pairs), 0) * slots
    lane = lax.broadcasted_iota(jnp.int32, (atoms, pairs), 1)
    diagonal = jnp.logical_and(lane >= row, lane < row + slots)
    rows = []
    for c in range(3):
        f = jnp.dot(both, deriv_ref[c], preferred_element_type=F32)
        f = jnp.where(diagonal, f[:atoms] + f[atoms:], 0.0)
        rows.append(jnp.sum(f, axis=0, keepdims=True))
    partial = jnp.concatenate(rows + [jnp.zeros((5, pairs), F32)], axis=0)
    first = partial.astype(BF16)
    rest = partial - first.astype(F32)
    second = rest.astype(BF16)
    third = (rest - second.astype(F32)).astype(BF16)
    pieces = jnp.concatenate([first.astype(F32), second.astype(F32), third.astype(F32)], axis=0)
    moved = jnp.dot(pieces.astype(BF16), table_ref[...], preferred_element_type=F32)
    out_ref[...] = moved[0:8] + moved[8:16] + moved[16:24]


def body(descriptors, sparse_points, coefficients, derivatives, neighbours, counts, ghost_index):
    yl, core = lax.axis_index("yl"), lax.axis_index("c")
    first = yl == 0
    owned, width = descriptors.shape
    points, part = sparse_points.shape
    n_sp, n_plane = lax.axis_size(SP), lax.axis_size(PLANE)
    n_chips = lax.axis_size(CHIPS)
    columns = n_sp * width
    half = points // 2
    slots_count = neighbours.shape[1]
    pairs_count = owned * slots_count
    ghosts = ghost_index.shape[0] // 2

    with jax.named_scope("points_swap"):
        turned = sparse_points.T
        one, two = turned[:, :half], turned[:, half:]
        got = lax.ppermute(jnp.where(first, two, one), "yl", [(0, 1), (1, 0)])
        swapped = jnp.concatenate(
            [jnp.where(first, one, got), jnp.where(first, got, two)], axis=0
        )
    with jax.named_scope("points_gather"):
        basis = lax.all_gather(swapped, "z", axis=0, tiled=True)

    with jax.named_scope("descriptors_gather"):
        spread = jnp.broadcast_to(descriptors[None], (n_plane, owned, width))
        blocks = lax.all_to_all(spread, PLANE, 0, 0).reshape(2, n_sp, owned, width)
        rows = jnp.transpose(blocks, (0, 2, 1, 3)).reshape(2 * owned, columns)
        values = rows.astype(F32)
        row_norm = jnp.sqrt(jnp.sum(values * values, axis=1, keepdims=True) + 1e-06)
        unit_rows = (values / row_norm).astype(BF16)
        scale = 1.0 / row_norm

    with jax.named_scope("scatter_table"):
        slot_total = owned + 2 * ghosts
        flat = neighbours.reshape(pairs_count)
        slot_ids = jnp.arange(slot_total, dtype=jnp.int32)
        hot = (flat[:, None] == slot_ids[None, :]).astype(BF16)
        target = jnp.concatenate(
            [
                jnp.arange(owned, dtype=jnp.int32),
                ghost_index[:ghosts] + owned,
                ghost_index[ghosts:] + 2 * owned,
            ]
        )
        column_ids = jnp.arange(3 * owned, dtype=jnp.int32)
        moves = (target[:, None] == column_ids[None, :]).astype(BF16)
        landed = jnp.dot(hot, moves, preferred_element_type=F32)
        atom_of = jnp.arange(pairs_count, dtype=jnp.int32) // slots_count
        slot_of = jnp.arange(pairs_count, dtype=jnp.int32) % slots_count
        self_hot = (atom_of[:, None] == column_ids[None, :]).astype(F32)
        live = slot_of < jnp.repeat(counts, slots_count)
        table = jnp.where(live[:, None], self_hot - landed, 0.0).astype(BF16)
        lined = jnp.transpose(derivatives, (1, 3, 0, 2)).reshape(3, width, pairs_count)

    with jax.named_scope("main"):
        mine = lax.dynamic_slice_in_dim(coefficients, yl * half, half, 0)[None, :]
        vmem = pl.BlockSpec(memory_space=pltpu.VMEM)
        share = jax.ShapeDtypeStruct((2, n_chips // 2, owned, width), F32)
        own, other, energy_part = pl.pallas_call(
            main_kernel,
            out_shape=(share, share, jax.ShapeDtypeStruct((2, 8, owned), F32)),
            in_specs=[
                pl.BlockSpec(memory_space=pltpu.SMEM),
                vmem,
                vmem,
                vmem,
                pl.BlockSpec(memory_space=pltpu.HBM),
            ],
            out_specs=(vmem, vmem, vmem),
            scratch_shapes=[
                pltpu.VMEM((columns, half), BF16),
                pltpu.VMEM((2 * owned, half), F32),
                pltpu.VMEM((2 * owned, half), BF16),
                pltpu.VMEM((2 * owned, 128), F32),
                pltpu.SemaphoreType.DMA((CHUNKS,)),
            ],
            compiler_params=pltpu.CompilerParams(vmem_limit_bytes=32 << 20),
            cost_estimate=pl.CostEstimate(
                flops=8 * owned * half * columns, bytes_accessed=8 << 20, transcendentals=0
            ),
        )(core.reshape(1).astype(jnp.int32), unit_rows, scale, mine, basis)
    with jax.named_scope("core_pair"):
        theirs = lax.ppermute(other, "c", [(0, 1), (1, 0)])
        outgoing = (own + theirs).astype(BF16).reshape(n_chips, owned, width)
    with jax.named_scope("gradient_exchange"):
        parts = lax.all_to_all(outgoing, CHIPS, 0, 0)
    with jax.named_scope("tail"):
        moved = pl.pallas_call(
            tail_kernel,
            out_shape=jax.ShapeDtypeStruct((8, 3 * owned), F32),
            in_specs=[vmem, vmem, vmem],
            out_specs=vmem,
            compiler_params=pltpu.CompilerParams(vmem_limit_bytes=24 << 20),
            cost_estimate=pl.CostEstimate(
                flops=12 * owned * width * pairs_count, bytes_accessed=4 << 20, transcendentals=0
            ),
        )(parts, lined, table)
        keep, to_left, to_right = jnp.split(moved[:3], 3, axis=1)
    with jax.named_scope("ghosts"):
        across = jnp.where(first, to_left, to_right)
        beside = jnp.where(first, to_right, to_left)
        size = lax.axis_size(DOM)
        pairs = [(i, (i - 1) % size if i % 2 == 0 else (i + 1) % size) for i in range(size)]
        keep = keep + lax.ppermute(across, DOM, pairs)
        both = jnp.stack([jnp.where(first, keep, beside), jnp.where(first, beside, keep)])
        both = jnp.concatenate([both, energy_part[:, :1]], axis=1)
        both = jnp.broadcast_to(both[:, None], (2, n_sp, 4, owned)).reshape(n_plane, 4, owned)
        received = jnp.sum(lax.all_to_all(both, PLANE, 0, 0), axis=0)
    return (received[:3], received[3])


def solution(mesh):
    grid = Mesh(mesh.devices.reshape(16, 2, 4, 2, 2), ("z", "yl", "x", "yh", "c"))
    return jax.shard_map(
        body,
        mesh=grid,
        in_specs=(
            P(DOM, SP),
            P(SP, DOM),
            P(SP),
            P(DOM, None, None, SP),
            P(DOM, None),
            P(DOM),
            P(DOM),
        ),
        out_specs=(P(None, DOM), P(DOM)),
        check_vma=False,
    )
```

```python
import jax
import jax.numpy as jnp
from jax import lax
from jax.experimental import pallas as pl
from jax.experimental.pallas import tpu as pltpu
from jax.sharding import Mesh, PartitionSpec as P

DOM = ("zh", "zl", "yl")
SP = ("x", "yh", "c")
QUARTER = ("zl", "yl")
CHIPS = ("zl", "yl", "x", "yh")
SLAB = ("zl", "yl", "x", "yh", "c")
F32, BF16 = jnp.float32, jnp.bfloat16
LAST = (((1,), (1,)), ((), ()))


def main_kernel(place_ref, unit_ref, scale_ref, coef_ref, *rest):
    (*blocks, own_ref, other_ref, energy_ref, basis, kernel, slopes, inner, scale) = rest
    depth = blocks[0].shape[0]
    atoms = unit_ref.shape[0]
    domains = energy_ref.shape[0]
    owned = atoms // domains
    for i, block in enumerate(blocks):
        at = pl.multiple_of(place_ref[1 + i] * depth, depth)
        basis[pl.ds(at, depth), :] = block[...]
    kernel[...] = jnp.dot(unit_ref[...], basis[...], preferred_element_type=F32)
    four = 4.0 * coef_ref[...]
    rows = 32
    for r in range(0, atoms, rows):
        k = kernel[r : r + rows, :]
        s = four * (k * k * k)
        low = s.astype(BF16)
        slopes[r : r + rows, :] = low
        wide = jnp.broadcast_to(scale_ref[r : r + rows, :], (rows, 128))
        scale[r : r + rows, :] = wide
        inner[r : r + rows, :] = wide * jnp.sum(low.astype(F32) * k, axis=1, keepdims=True)
        kernel[r : r + rows, 0:128] = jnp.broadcast_to(
            0.25 * jnp.sum(s * k, axis=1, keepdims=True), (rows, 128)
        )
    for y in range(domains):
        energy_ref[y] = kernel[y * owned : (y + 1) * owned, 0:128].T[0:8, :]
    even_first = place_ref[0] == 0
    for j in range(len(blocks)):
        g = lax.dot_general(
            slopes[...],
            basis[j * depth : (j + 1) * depth, :],
            LAST,
            preferred_element_type=F32,
        )
        for p in range(2):
            lanes = slice(j * depth + p * 128, j * depth + (p + 1) * 128)
            u = unit_ref[:, lanes].astype(F32)
            part = g[:, p * 128 : (p + 1) * 128] * scale[...] - u * inner[...]

            @pl.when(even_first if p == 0 else jnp.logical_not(even_first))
            def _():
                for y in range(domains):
                    own_ref[y, j] = part[y * owned : (y + 1) * owned]

            @pl.when(jnp.logical_not(even_first) if p == 0 else even_first)
            def _():
                for y in range(domains):
                    other_ref[y, j] = part[y * owned : (y + 1) * owned]


def tail_kernel(parts_ref, deriv_ref, table_ref, out_ref):
    total = parts_ref[0].astype(F32)
    for i in range(1, parts_ref.shape[0]):
        total += parts_ref[i].astype(F32)
    atoms = total.shape[0]
    pairs = deriv_ref.shape[2]
    high = total.astype(BF16)
    low = (total - high.astype(F32)).astype(BF16)
    both = jnp.concatenate([high, low], axis=0)
    slots = pairs // atoms
    row = lax.broadcasted_iota(jnp.int32, (atoms, pairs), 0) * slots
    lane = lax.broadcasted_iota(jnp.int32, (atoms, pairs), 1)
    diagonal = jnp.logical_and(lane >= row, lane < row + slots)
    rows = []
    for c in range(3):
        f = jnp.dot(both, deriv_ref[c], preferred_element_type=F32)
        f = jnp.where(diagonal, f[:atoms] + f[atoms:], 0.0)
        rows.append(jnp.sum(f, axis=0, keepdims=True))
    partial = jnp.concatenate(rows + [jnp.zeros((5, pairs), F32)], axis=0)
    first = partial.astype(BF16)
    rest = partial - first.astype(F32)
    second = rest.astype(BF16)
    third = (rest - second.astype(F32)).astype(BF16)
    pieces = jnp.concatenate([first.astype(F32), second.astype(F32), third.astype(F32)], axis=0)
    moved = jnp.dot(pieces.astype(BF16), table_ref[...], preferred_element_type=F32)
    out_ref[...] = moved[0:8] + moved[8:16] + moved[16:24]


def body(descriptors, sparse_points, coefficients, derivatives, neighbours, counts, ghost_index):
    core = lax.axis_index("c")
    quarter = lax.axis_index(QUARTER)
    slab = lax.axis_index("zh")
    owned, width = descriptors.shape
    points, part = sparse_points.shape
    n_sp, n_chips, n_slab = (lax.axis_size(SP), lax.axis_size(CHIPS), lax.axis_size(SLAB))
    n_quarter, n_ring = lax.axis_size(QUARTER), lax.axis_size("zh")
    columns = n_sp * width
    share = points // n_quarter
    atoms = n_quarter * owned
    slots_count = neighbours.shape[1]
    pairs_count = owned * slots_count
    ghosts = ghost_index.shape[0] // 2
    swap = [(0, 1), (1, 0)]

    with jax.named_scope("points_swap"):
        split = jnp.transpose(sparse_points.T.reshape(part, n_quarter, share), (1, 0, 2))
        block = lax.all_to_all(split, QUARTER, 0, 0).reshape(n_quarter * part, share)
    with jax.named_scope("points_ring"):
        up = [(i, (i + 1) % n_ring) for i in range(n_ring)]
        down = [(i, (i - 1) % n_ring) for i in range(n_ring)]
        blocks, places = [block], [slab]
        above = below = block
        for step in range(1, n_ring // 2 + 1):
            above = lax.ppermute(above, "zh", up)
            blocks.append(above)
            places.append((slab - step) % n_ring)
            if step < n_ring // 2:
                below = lax.ppermute(below, "zh", down)
                blocks.append(below)
                places.append((slab + step) % n_ring)
            if step == 2:
                middle = above

    with jax.named_scope("descriptors_gather"):
        spread = jnp.broadcast_to(descriptors[None], (n_chips, owned, width))
        spread, _ = lax.optimization_barrier((spread, block))
        mine = lax.all_to_all(spread, CHIPS, 0, 0)
        mine, _ = lax.optimization_barrier((mine, middle))
        theirs = lax.ppermute(mine, "c", swap)
        even, odd = jnp.where(core == 0, mine, theirs), jnp.where(core == 0, theirs, mine)
        halves = jnp.stack([even, odd]).reshape(2, n_quarter, n_sp // 2, owned, width)
        rows = jnp.transpose(halves, (1, 3, 2, 0, 4)).reshape(atoms, columns)
        values = rows.astype(F32)
        row_norm = jnp.sqrt(jnp.sum(values * values, axis=1, keepdims=True) + 1e-06)
        unit_rows = (values / row_norm).astype(BF16)
        scale = 1.0 / row_norm

    with jax.named_scope("scatter_table"):
        slot_total = owned + 2 * ghosts
        flat = neighbours.reshape(pairs_count)
        slot_ids = jnp.arange(slot_total, dtype=jnp.int32)
        hot = (flat[:, None] == slot_ids[None, :]).astype(BF16)
        target = jnp.concatenate(
            [
                jnp.arange(owned, dtype=jnp.int32),
                ghost_index[:ghosts] + owned,
                ghost_index[ghosts:] + 2 * owned,
            ]
        )
        column_ids = jnp.arange(3 * owned, dtype=jnp.int32)
        moves = (target[:, None] == column_ids[None, :]).astype(BF16)
        landed = jnp.dot(hot, moves, preferred_element_type=F32)
        atom_of = jnp.arange(pairs_count, dtype=jnp.int32) // slots_count
        slot_of = jnp.arange(pairs_count, dtype=jnp.int32) % slots_count
        self_hot = (atom_of[:, None] == column_ids[None, :]).astype(F32)
        live = slot_of < jnp.repeat(counts, slots_count)
        table = jnp.where(live[:, None], self_hot - landed, 0.0).astype(BF16)
        lined = jnp.transpose(derivatives, (1, 3, 0, 2)).reshape(3, width, pairs_count)

    unit_rows, scale, table, lined = lax.optimization_barrier((unit_rows, scale, table, lined))
    with jax.named_scope("main"):
        coefs = lax.dynamic_slice_in_dim(coefficients, quarter * share, share, 0)[None, :]
        vmem = pl.BlockSpec(memory_space=pltpu.VMEM)
        piece = jax.ShapeDtypeStruct((n_quarter, n_sp // 2, owned, width), F32)
        own, other, energy_part = pl.pallas_call(
            main_kernel,
            out_shape=(piece, piece, jax.ShapeDtypeStruct((n_quarter, 8, owned), F32)),
            in_specs=[pl.BlockSpec(memory_space=pltpu.SMEM)] + [vmem] * (3 + len(blocks)),
            out_specs=(vmem, vmem, vmem),
            scratch_shapes=[
                pltpu.VMEM((columns, share), BF16),
                pltpu.VMEM((atoms, share), F32),
                pltpu.VMEM((atoms, share), BF16),
                pltpu.VMEM((atoms, 128), F32),
                pltpu.VMEM((atoms, 128), F32),
            ],
            compiler_params=pltpu.CompilerParams(vmem_limit_bytes=32 << 20),
            cost_estimate=pl.CostEstimate(
                flops=4 * atoms * share * columns, bytes_accessed=8 << 20, transcendentals=0
            ),
        )(jnp.stack([core] + places).astype(jnp.int32), unit_rows, scale, coefs, *blocks)
    with jax.named_scope("core_pair"):
        outgoing = (own + lax.ppermute(other, "c", swap)).astype(BF16)
        outgoing = outgoing.reshape(n_chips, owned, width)
    with jax.named_scope("gradient_exchange"):
        parts = lax.all_to_all(outgoing, CHIPS, 0, 0)
    with jax.named_scope("tail"):
        moved = pl.pallas_call(
            tail_kernel,
            out_shape=jax.ShapeDtypeStruct((8, 3 * owned), F32),
            in_specs=[vmem, vmem, vmem],
            out_specs=vmem,
            compiler_params=pltpu.CompilerParams(vmem_limit_bytes=24 << 20),
            cost_estimate=pl.CostEstimate(
                flops=12 * owned * width * pairs_count, bytes_accessed=4 << 20, transcendentals=0
            ),
        )(parts, lined, table)
        keep, to_left, to_right = jnp.split(moved[:3], 3, axis=1)
    with jax.named_scope("ghosts"):
        lowest = quarter == 0
        size = lax.axis_size(DOM)
        pairs = [(i, (i - 1) % size) for i in range(0, size, n_quarter)]
        pairs += [(i, (i + 1) % size) for i in range(n_quarter - 1, size, n_quarter)]
        keep = keep + lax.ppermute(jnp.where(lowest, to_left, to_right), DOM, pairs)
        to = jnp.arange(n_quarter, dtype=jnp.int32)[:, None, None]
        sent = jnp.where(to == quarter, keep, 0.0)
        sent = jnp.where(to == quarter - 1, to_left, sent)
        sent = jnp.where(to == quarter + 1, to_right, sent)
        sent = jnp.concatenate([sent, energy_part[:, :1]], axis=1)
        sent = jnp.broadcast_to(sent[:, None], (n_quarter, n_sp, 4, owned))
        received = lax.all_to_all(sent.reshape(n_slab, 4, owned), SLAB, 0, 0)
        received = jnp.sum(received, axis=0)
    return (received[:3], received[3])


def solution(mesh):
    grid = Mesh(
        mesh.devices.reshape(8, 2, 2, 4, 2, 2), ("zh", "zl", "yl", "x", "yh", "c")
    )
    return jax.shard_map(
        body,
        mesh=grid,
        in_specs=(
            P(DOM, SP),
            P(SP, DOM),
            P(SP),
            P(DOM, None, None, SP),
            P(DOM, None),
            P(DOM),
            P(DOM),
        ),
        out_specs=(P(None, DOM), P(DOM)),
        check_vma=False,
    )
```

```python
import jax
import jax.numpy as jnp
from jax import lax
from jax.experimental import pallas as pl
from jax.experimental.pallas import tpu as pltpu
from jax.sharding import Mesh, PartitionSpec as P

DOM = ("z", "yl")
SP = ("x", "yh", "c")
PLANE = ("yl", "x", "yh", "c")
LIFT = 4096.0
F32, BF16, F16 = jnp.float32, jnp.bfloat16, jnp.float16
LAST = (((1,), (1,)), ((), ()))


def spread_kernel(rows_ref, out_hbm, sems):
    copies = [
        pltpu.make_async_copy(rows_ref, out_hbm.at[i], sems.at[i]) for i in range(out_hbm.shape[0])
    ]
    for copy in copies:
        copy.start()
    for copy in copies:
        copy.wait()


def prepare_kernel(side_ref, rows_ref, unit_ref, scale_ref):
    domains = 2
    blocks = rows_ref.shape[0] // domains
    owned, width = rows_ref.shape[1:]
    shift = side_ref[0] * (width // 2)
    for y in range(domains):
        total = jnp.zeros((owned, width), F32)
        for s in range(blocks):
            value = rows_ref[y * blocks + s].astype(F32)
            total += value * value
        norm = jnp.sqrt(jnp.sum(total, axis=1, keepdims=True) + 1e-06)
        scale = jnp.broadcast_to(1.0 / norm, (owned, width))
        scale_ref[y * owned : (y + 1) * owned, :] = scale
        for s in range(blocks):
            value = rows_ref[y * blocks + s].astype(F32) * scale
            unit_ref[y * owned : (y + 1) * owned, s * width : (s + 1) * width] = pltpu.roll(
                value, shift, 1
            ).astype(BF16)


def main_kernel(unit, scale_ref, coef_ref, basis, share_ref, energy_ref, kernel, slopes, inner):
    columns = basis.shape[0]
    width = scale_ref.shape[1]
    atoms = unit.shape[0]
    domains = energy_ref.shape[0]
    owned = atoms // domains
    blocks = columns // width
    kernel[...] = jnp.dot(unit[...], basis[...], preferred_element_type=F32)
    four = 4.0 * coef_ref[...]
    rows = 32
    for r in range(0, atoms, rows):
        k = kernel[r : r + rows, :]
        s = four * (k * k * k)
        low = s.astype(BF16)
        slopes[r : r + rows, :] = low
        inner[r : r + rows, :] = scale_ref[r : r + rows, :] * jnp.sum(
            low.astype(F32) * k, axis=1, keepdims=True
        )
        kernel[r : r + rows, 0:128] = jnp.broadcast_to(
            0.25 * jnp.sum(s * k, axis=1, keepdims=True), (rows, 128)
        )
    for y in range(domains):
        energy_ref[y] = kernel[y * owned : (y + 1) * owned, 0:128].T[0:8, :]
    for i in range(0, blocks, 2):
        g = lax.dot_general(
            slopes[...],
            basis[i * width : (i + 2) * width, :],
            LAST,
            preferred_element_type=F32,
        )
        for p in range(2):
            lanes = slice((i + p) * width, (i + p + 1) * width)
            part = (
                g[:, p * width : (p + 1) * width] * scale_ref[...]
                - unit[:, lanes].astype(F32) * inner[...]
            ).astype(BF16)
            for y in range(domains):
                share_ref[y * blocks + i + p] = part[y * owned : (y + 1) * owned]


def tail_kernel(parts_ref, deriv_ref, table_ref, out_ref):
    count, atoms, width = parts_ref.shape
    sides = []
    for y in range(2):
        total = parts_ref[y * (count // 2)].astype(F32)
        for i in range(1, count // 2):
            total += parts_ref[y * (count // 2) + i].astype(F32)
        sides.append(total)
    total = sides[0] + pltpu.roll(sides[1], width // 2, 1)
    pairs = deriv_ref.shape[1]
    high = total.astype(BF16)
    low = (total - high.astype(F32)).astype(BF16)
    both = jnp.concatenate([high, low], axis=0)
    row = lax.broadcasted_iota(jnp.int32, (atoms, pairs), 0)
    lane = lax.broadcasted_iota(jnp.int32, (atoms, pairs), 1)
    diagonal = row == lane % atoms
    rows = []
    for c in range(3):
        f = lax.dot_general(both, deriv_ref[c], LAST, preferred_element_type=F32)
        f = jnp.where(diagonal, f[:atoms] + f[atoms:], 0.0)
        rows.append(jnp.sum(f, axis=0, keepdims=True))
    partial = jnp.concatenate(rows + [jnp.zeros((5, pairs), F32)], axis=0)
    first = partial.astype(BF16)
    rest = partial - first.astype(F32)
    second = rest.astype(BF16)
    third = (rest - second.astype(F32)).astype(BF16)
    pieces = jnp.concatenate([first.astype(F32), second.astype(F32), third.astype(F32)], axis=0)
    moved = jnp.dot(pieces.astype(BF16), table_ref[...], preferred_element_type=F32)
    out_ref[...] = moved[0:8] + moved[8:16] + moved[16:24]


def body(descriptors, sparse_points, coefficients, derivatives, neighbours, counts, ghost_index):
    yl = lax.axis_index("yl")
    first = yl == 0
    owned, width = descriptors.shape
    points, part = sparse_points.shape
    n_sp, n_plane = lax.axis_size(SP), lax.axis_size(PLANE)
    columns = n_sp * width
    half = points // 2
    atoms = 2 * owned
    slots_count = neighbours.shape[1]
    pairs_count = owned * slots_count
    ghosts = ghost_index.shape[0] // 2
    swap = [(0, 1), (1, 0)]
    vmem = pl.BlockSpec(memory_space=pltpu.VMEM)
    smem = pl.BlockSpec(memory_space=pltpu.SMEM)
    anywhere = pl.BlockSpec(memory_space=pl.ANY)

    with jax.named_scope("points_swap"):
        turned = sparse_points.T
        kept = lax.dynamic_slice_in_dim(turned, yl * half, half, 1).astype(F32) * LIFT
        sent = lax.dynamic_slice_in_dim(turned, (1 - yl) * half, half, 1).astype(F32) * LIFT
        got = lax.ppermute(sent.astype(F16), "yl", swap)
        block = jnp.concatenate([kept.astype(F16), got], axis=0)
    with jax.named_scope("points_gather"):
        lifted = lax.all_gather(block, "z", axis=0, tiled=True)
        basis = (lifted.astype(F32) * (1.0 / LIFT)).astype(BF16)

    with jax.named_scope("descriptors_gather"):
        spread = pl.pallas_call(
            spread_kernel,
            out_shape=jax.ShapeDtypeStruct((n_plane, owned, width), BF16),
            in_specs=[vmem],
            out_specs=anywhere,
            scratch_shapes=[pltpu.SemaphoreType.DMA((n_plane,))],
            compiler_params=pltpu.CompilerParams(vmem_limit_bytes=4 << 20),
        )(descriptors)
        spread, block = lax.optimization_barrier((spread, block))
        rows = lax.all_to_all(spread, PLANE, 0, 0)
        unit_rows, scale = pl.pallas_call(
            prepare_kernel,
            out_shape=(
                jax.ShapeDtypeStruct((atoms, columns), BF16),
                jax.ShapeDtypeStruct((atoms, width), F32),
            ),
            in_specs=[smem, vmem],
            out_specs=(vmem, vmem),
            compiler_params=pltpu.CompilerParams(vmem_limit_bytes=16 << 20),
            cost_estimate=pl.CostEstimate(
                flops=8 * atoms * columns, bytes_accessed=4 << 20, transcendentals=0
            ),
        )(yl.reshape(1).astype(jnp.int32), rows)

    with jax.named_scope("scatter_table"):
        slot_total = owned + 2 * ghosts
        flat = neighbours.T.reshape(pairs_count)
        slot_ids = jnp.arange(slot_total, dtype=jnp.int32)
        hot = (flat[:, None] == slot_ids[None, :]).astype(BF16)
        target = jnp.concatenate(
            [
                jnp.arange(owned, dtype=jnp.int32),
                ghost_index[:ghosts] + owned,
                ghost_index[ghosts:] + 2 * owned,
            ]
        )
        column_ids = jnp.arange(3 * owned, dtype=jnp.int32)
        moves = (target[:, None] == column_ids[None, :]).astype(BF16)
        landed = jnp.dot(hot, moves, preferred_element_type=F32)
        atom_of = jnp.arange(pairs_count, dtype=jnp.int32) % owned
        slot_of = jnp.arange(pairs_count, dtype=jnp.int32) // owned
        self_hot = (atom_of[:, None] == column_ids[None, :]).astype(F32)
        live = slot_of < jnp.tile(counts, slots_count)
        table = jnp.where(live[:, None], self_hot - landed, 0.0).astype(BF16)
        lined = jnp.transpose(derivatives, (1, 2, 0, 3)).reshape(3, pairs_count, width)

    unit_rows, scale, table = lax.optimization_barrier((unit_rows, scale, table))
    with jax.named_scope("main"):
        coefs = lax.dynamic_slice_in_dim(coefficients, yl * half, half, 0)[None, :]
        outgoing, energy_part = pl.pallas_call(
            main_kernel,
            out_shape=(
                jax.ShapeDtypeStruct((n_plane, owned, width), BF16),
                jax.ShapeDtypeStruct((2, 8, owned), F32),
            ),
            in_specs=[vmem] * 4,
            out_specs=(vmem, vmem),
            scratch_shapes=[
                pltpu.VMEM((atoms, half), F32),
                pltpu.VMEM((atoms, half), BF16),
                pltpu.VMEM((atoms, width), F32),
            ],
            compiler_params=pltpu.CompilerParams(vmem_limit_bytes=24 << 20),
            cost_estimate=pl.CostEstimate(
                flops=4 * atoms * half * columns, bytes_accessed=8 << 20, transcendentals=0
            ),
        )(unit_rows, scale, coefs, basis)
    with jax.named_scope("gradient_exchange"):
        parts = lax.all_to_all(outgoing, PLANE, 0, 0)
    with jax.named_scope("tail"):
        moved = pl.pallas_call(
            tail_kernel,
            out_shape=jax.ShapeDtypeStruct((8, 3 * owned), F32),
            in_specs=[vmem, vmem, vmem],
            out_specs=vmem,
            compiler_params=pltpu.CompilerParams(vmem_limit_bytes=24 << 20),
            cost_estimate=pl.CostEstimate(
                flops=12 * owned * width * pairs_count, bytes_accessed=4 << 20, transcendentals=0
            ),
        )(parts, lined, table)
        keep, to_left, to_right = jnp.split(moved[:3], 3, axis=1)
    with jax.named_scope("ghosts"):
        across = jnp.where(first, to_left, to_right)
        beside = jnp.where(first, to_right, to_left)
        size = lax.axis_size(DOM)
        pairs = [(i, (i - 1) % size if i % 2 == 0 else (i + 1) % size) for i in range(size)]
        keep = keep + lax.ppermute(across, DOM, pairs)
        both = jnp.stack([jnp.where(first, keep, beside), jnp.where(first, beside, keep)])
        both = jnp.concatenate([both, energy_part[:, :1]], axis=1)
        both = jnp.broadcast_to(both[:, None], (2, n_sp, 4, owned)).reshape(n_plane, 4, owned)
        received = jnp.sum(lax.all_to_all(both, PLANE, 0, 0), axis=0)
    return (received[:3], received[3])


def solution(mesh):
    grid = Mesh(mesh.devices.reshape(16, 2, 4, 2, 2), ("z", "yl", "x", "yh", "c"))
    return jax.shard_map(
        body,
        mesh=grid,
        in_specs=(
            P(DOM, SP),
            P(SP, DOM),
            P(SP),
            P(DOM, None, None, SP),
            P(DOM, None),
            P(DOM),
            P(DOM),
        ),
        out_specs=(P(None, DOM), P(DOM)),
        check_vma=False,
    )
```

```python
import jax
import jax.numpy as jnp
from jax import lax
from jax.experimental import pallas as pl
from jax.experimental.pallas import tpu as pltpu
from jax.sharding import Mesh, PartitionSpec as P

DOM = ("z", "yl")
SP = ("x", "yh", "c")
PLANE = ("yl", "x", "yh", "c")
LIFT = 4096.0
F32, BF16, F16 = jnp.float32, jnp.bfloat16, jnp.float16
LAST = (((1,), (1,)), ((), ()))


def spread_kernel(rows_ref, out_hbm, sems):
    copies = [
        pltpu.make_async_copy(rows_ref, out_hbm.at[i], sems.at[i]) for i in range(out_hbm.shape[0])
    ]
    for copy in copies:
        copy.start()
    for copy in copies:
        copy.wait()


def prepare_kernel(side_ref, rows_ref, unit_ref, scale_ref):
    domains = 2
    blocks = rows_ref.shape[0] // domains
    owned, width = rows_ref.shape[1:]
    shift = side_ref[0] * (width // 2)
    for y in range(domains):
        total = jnp.zeros((owned, width), F32)
        for s in range(blocks):
            value = rows_ref[y * blocks + s].astype(F32)
            total += value * value
        norm = jnp.sqrt(jnp.sum(total, axis=1, keepdims=True) + 1e-06)
        scale = jnp.broadcast_to(1.0 / norm, (owned, width))
        scale_ref[y * owned : (y + 1) * owned, :] = scale
        for s in range(blocks):
            value = rows_ref[y * blocks + s].astype(F32) * (scale * (1.0 / LIFT))
            unit_ref[y * owned : (y + 1) * owned, s * width : (s + 1) * width] = pltpu.roll(
                value, shift, 1
            ).astype(BF16)


def slope_kernel(side_ref, kernel_ref, scale_ref, coef_ref, slopes_ref, inner_ref, energy_ref, wide):
    atoms = kernel_ref.shape[0]
    domains = energy_ref.shape[0]
    owned = atoms // domains
    four = 4.0 * coef_ref[pl.ds(side_ref[0], 1), :]
    rows = 32
    for r in range(0, atoms, rows):
        k = kernel_ref[r : r + rows, :]
        s = four * (k * k * k)
        low = s.astype(BF16)
        slopes_ref[r : r + rows, :] = low
        inner_ref[r : r + rows, :] = (scale_ref[r : r + rows, :] * LIFT) * jnp.sum(
            low.astype(F32) * k, axis=1, keepdims=True
        )
        wide[r : r + rows, :] = jnp.broadcast_to(
            0.25 * jnp.sum(s * k, axis=1, keepdims=True), (rows, 128)
        )
    for y in range(domains):
        energy_ref[y] = wide[y * owned : (y + 1) * owned, :].T[0:8, :]


def project_kernel(gradient_ref, unit_ref, scale_ref, inner_ref, share_hbm, share, sems):
    count, owned, width = share.shape
    domains = unit_ref.shape[0] // owned
    blocks = count // domains
    scale = scale_ref[...] * (1.0 / LIFT)
    sends = []
    for i in range(0, blocks, 4):
        for p in range(i, i + 4):
            lanes = slice(p * width, (p + 1) * width)
            part = (
                gradient_ref[:, lanes] * scale - unit_ref[:, lanes].astype(F32) * inner_ref[...]
            ).astype(BF16)
            for y in range(domains):
                share[y * blocks + p] = part[y * owned : (y + 1) * owned]
        for y in range(domains):
            at = pl.ds(y * blocks + i, 4)
            sends.append(pltpu.make_async_copy(share.at[at], share_hbm.at[at], sems.at[len(sends)]))
            sends[-1].start()
    for send in sends:
        send.wait()


def tail_kernel(parts_ref, deriv_ref, table_ref, out_ref):
    count, atoms, width = parts_ref.shape
    sides = []
    for y in range(2):
        total = parts_ref[y * (count // 2)].astype(F32)
        for i in range(1, count // 2):
            total += parts_ref[y * (count // 2) + i].astype(F32)
        sides.append(total)
    total = sides[0] + pltpu.roll(sides[1], width // 2, 1)
    pairs = deriv_ref.shape[1]
    high = total.astype(BF16)
    low = (total - high.astype(F32)).astype(BF16)
    both = jnp.concatenate([high, low], axis=0)
    row = lax.broadcasted_iota(jnp.int32, (atoms, pairs), 0)
    lane = lax.broadcasted_iota(jnp.int32, (atoms, pairs), 1)
    diagonal = row == lane % atoms
    rows = []
    for c in range(3):
        f = lax.dot_general(both, deriv_ref[c], LAST, preferred_element_type=F32)
        f = jnp.where(diagonal, f[:atoms] + f[atoms:], 0.0)
        rows.append(jnp.sum(f, axis=0, keepdims=True))
    partial = jnp.concatenate(rows + [jnp.zeros((5, pairs), F32)], axis=0)
    first = partial.astype(BF16)
    rest = partial - first.astype(F32)
    second = rest.astype(BF16)
    third = (rest - second.astype(F32)).astype(BF16)
    pieces = jnp.concatenate([first.astype(F32), second.astype(F32), third.astype(F32)], axis=0)
    moved = jnp.dot(pieces.astype(BF16), table_ref[...], preferred_element_type=F32)
    out_ref[...] = moved[0:8] + moved[8:16] + moved[16:24]


def body(descriptors, sparse_points, coefficients, derivatives, neighbours, counts, ghost_index):
    yl = lax.axis_index("yl")
    first = yl == 0
    owned, width = descriptors.shape
    points, part = sparse_points.shape
    n_sp, n_plane = lax.axis_size(SP), lax.axis_size(PLANE)
    columns = n_sp * width
    half = points // 2
    atoms = 2 * owned
    slots_count = neighbours.shape[1]
    pairs_count = owned * slots_count
    ghosts = ghost_index.shape[0] // 2
    swap = [(0, 1), (1, 0)]
    vmem = pl.BlockSpec(memory_space=pltpu.VMEM)
    smem = pl.BlockSpec(memory_space=pltpu.SMEM)
    anywhere = pl.BlockSpec(memory_space=pl.ANY)

    side = yl.reshape(1).astype(jnp.int32)

    with jax.named_scope("points_swap"):
        turned = sparse_points.T
        kept = lax.dynamic_slice_in_dim(turned, yl * half, half, 1).astype(F32) * LIFT
        sent = lax.dynamic_slice_in_dim(turned, (1 - yl) * half, half, 1).astype(F32) * LIFT
        got = lax.ppermute(sent.astype(F16), "yl", swap)
        block = jnp.concatenate([kept.astype(F16), got], axis=0)
    with jax.named_scope("points_gather"):
        lifted = lax.all_gather(block, "z", axis=0, tiled=True)

    with jax.named_scope("descriptors_gather"):
        spread = pl.pallas_call(
            spread_kernel,
            out_shape=jax.ShapeDtypeStruct((n_plane, owned, width), BF16),
            in_specs=[anywhere],
            out_specs=anywhere,
            scratch_shapes=[pltpu.SemaphoreType.DMA((n_plane,))],
            compiler_params=pltpu.CompilerParams(vmem_limit_bytes=4 << 20),
        )(descriptors)
        rows = lax.all_to_all(spread, PLANE, 0, 0)
        unit_rows, scale = pl.pallas_call(
            prepare_kernel,
            out_shape=(
                jax.ShapeDtypeStruct((atoms, columns), BF16),
                jax.ShapeDtypeStruct((atoms, width), F32),
            ),
            in_specs=[smem, vmem],
            out_specs=(vmem, vmem),
            compiler_params=pltpu.CompilerParams(vmem_limit_bytes=16 << 20),
            cost_estimate=pl.CostEstimate(
                flops=8 * atoms * columns, bytes_accessed=4 << 20, transcendentals=0
            ),
        )(side, rows)

    with jax.named_scope("kernel"):
        kernel = jnp.dot(unit_rows, lifted.astype(BF16), preferred_element_type=F32)
        slopes, inner, energy_part = pl.pallas_call(
            slope_kernel,
            out_shape=(
                jax.ShapeDtypeStruct((atoms, half), BF16),
                jax.ShapeDtypeStruct((atoms, width), F32),
                jax.ShapeDtypeStruct((2, 8, owned), F32),
            ),
            in_specs=[smem] + [vmem] * 3,
            out_specs=(vmem, vmem, vmem),
            scratch_shapes=[pltpu.VMEM((atoms, width), F32)],
            compiler_params=pltpu.CompilerParams(vmem_limit_bytes=8 << 20),
        )(side, kernel, scale, coefficients.reshape(2, half))
    with jax.named_scope("gradient"):
        slopes, again = lax.optimization_barrier((slopes, lifted))
        gradient = lax.dot_general(
            slopes, again.astype(BF16), LAST, preferred_element_type=F32
        )
        outgoing = pl.pallas_call(
            project_kernel,
            out_shape=jax.ShapeDtypeStruct((n_plane, owned, width), BF16),
            in_specs=[vmem] * 4,
            out_specs=anywhere,
            scratch_shapes=[
                pltpu.VMEM((n_plane, owned, width), BF16),
                pltpu.SemaphoreType.DMA((8,)),
            ],
            compiler_params=pltpu.CompilerParams(vmem_limit_bytes=8 << 20),
        )(gradient, unit_rows, scale, inner)
    with jax.named_scope("gradient_exchange"):
        parts = lax.all_to_all(outgoing, PLANE, 0, 0)

    with jax.named_scope("scatter_table"):
        neighbours, counts, ghost_index, energy_part = lax.optimization_barrier(
            (neighbours, counts, ghost_index, energy_part)
        )
        slot_total = owned + 2 * ghosts
        flat = neighbours.T.reshape(pairs_count)
        slot_ids = jnp.arange(slot_total, dtype=jnp.int32)
        hot = (flat[:, None] == slot_ids[None, :]).astype(BF16)
        target = jnp.concatenate(
            [
                jnp.arange(owned, dtype=jnp.int32),
                ghost_index[:ghosts] + owned,
                ghost_index[ghosts:] + 2 * owned,
            ]
        )
        column_ids = jnp.arange(3 * owned, dtype=jnp.int32)
        moves = (target[:, None] == column_ids[None, :]).astype(BF16)
        landed = jnp.dot(hot, moves, preferred_element_type=F32)
        atom_of = jnp.arange(pairs_count, dtype=jnp.int32) % owned
        slot_of = jnp.arange(pairs_count, dtype=jnp.int32) // owned
        self_hot = (atom_of[:, None] == column_ids[None, :]).astype(F32)
        live = slot_of < jnp.tile(counts, slots_count)
        table = jnp.where(live[:, None], self_hot - landed, 0.0).astype(BF16)
        lined = jnp.transpose(derivatives, (1, 2, 0, 3)).reshape(3, pairs_count, width)

    with jax.named_scope("tail"):
        moved = pl.pallas_call(
            tail_kernel,
            out_shape=jax.ShapeDtypeStruct((8, 3 * owned), F32),
            in_specs=[vmem, vmem, vmem],
            out_specs=vmem,
            compiler_params=pltpu.CompilerParams(vmem_limit_bytes=24 << 20),
            cost_estimate=pl.CostEstimate(
                flops=12 * owned * width * pairs_count, bytes_accessed=4 << 20, transcendentals=0
            ),
        )(parts, lined, table)
        keep, to_left, to_right = jnp.split(moved[:3], 3, axis=1)
    with jax.named_scope("ghosts"):
        across = jnp.where(first, to_left, to_right)
        beside = jnp.where(first, to_right, to_left)
        size = lax.axis_size(DOM)
        pairs = [(i, (i - 1) % size if i % 2 == 0 else (i + 1) % size) for i in range(size)]
        keep = keep + lax.ppermute(across, DOM, pairs)
        both = jnp.stack([jnp.where(first, keep, beside), jnp.where(first, beside, keep)])
        both = jnp.concatenate([both, energy_part[:, :1]], axis=1)
        both = jnp.broadcast_to(both[:, None], (2, n_sp, 4, owned)).reshape(n_plane, 4, owned)
        received = jnp.sum(lax.all_to_all(both, PLANE, 0, 0), axis=0)
    return (received[:3], received[3])


def solution(mesh):
    grid = Mesh(mesh.devices.reshape(16, 2, 4, 2, 2), ("z", "yl", "x", "yh", "c"))
    return jax.shard_map(
        body,
        mesh=grid,
        in_specs=(
            P(DOM, SP),
            P(SP, DOM),
            P(SP),
            P(DOM, None, None, SP),
            P(DOM, None),
            P(DOM),
            P(DOM),
        ),
        out_specs=(P(None, DOM), P(DOM)),
        check_vma=False,
    )
```

```python
import jax
import jax.numpy as jnp
from jax import lax
from jax.experimental import pallas as pl
from jax.experimental.pallas import tpu as pltpu
from jax.sharding import Mesh, PartitionSpec as P

DOM = ("z", "yl")
SP = ("x", "yh", "c")
RUN = 4
PLANE = ("x", "yl", "yh", "c")
LIFT = 8192.0
F32, BF16, F16 = jnp.float32, jnp.bfloat16, jnp.float16
LAST = (((1,), (1,)), ((), ()))


def spread_kernel(rows_ref, out_hbm, sems):
    copies = [
        pltpu.make_async_copy(rows_ref, out_hbm.at[i], sems.at[i]) for i in range(out_hbm.shape[0])
    ]
    for copy in copies:
        copy.start()
    for copy in copies:
        copy.wait()


def prepare_kernel(side_ref, rows_ref, unit_ref, scale_ref):
    domains = 2
    blocks = rows_ref.shape[0] // domains
    owned, width = rows_ref.shape[1:]
    at = [[s // RUN * 2 * RUN + y * RUN + s % RUN for s in range(blocks)] for y in range(domains)]
    shift = side_ref[0] * (width // 2)
    for y in range(domains):
        total = jnp.zeros((owned, width), F32)
        for s in range(blocks):
            value = rows_ref[at[y][s]].astype(F32)
            total += value * value
        norm = jnp.sqrt(jnp.sum(total, axis=1, keepdims=True) + 1e-06)
        scale = jnp.broadcast_to(1.0 / norm, (owned, width))
        scale_ref[y * owned : (y + 1) * owned, :] = scale
        for s in range(blocks):
            value = rows_ref[at[y][s]].astype(F32) * (scale * (1.0 / LIFT))
            unit_ref[y * owned : (y + 1) * owned, s * width : (s + 1) * width] = pltpu.roll(
                value, shift, 1
            ).astype(BF16)


def slope_kernel(side_ref, kernel_ref, scale_ref, coef_ref, slopes_ref, inner_ref, energy_ref, wide):
    atoms = kernel_ref.shape[0]
    domains = energy_ref.shape[0]
    owned = atoms // domains
    four = 4.0 * coef_ref[pl.ds(side_ref[0], 1), :]
    rows = 32
    for r in range(0, atoms, rows):
        k = kernel_ref[r : r + rows, :]
        s = four * (k * k * k)
        low = s.astype(BF16)
        slopes_ref[r : r + rows, :] = low
        inner_ref[r : r + rows, :] = (scale_ref[r : r + rows, :] * LIFT) * jnp.sum(
            low.astype(F32) * k, axis=1, keepdims=True
        )
        wide[r : r + rows, :] = jnp.broadcast_to(
            0.25 * jnp.sum(s * k, axis=1, keepdims=True), (rows, 128)
        )
    for y in range(domains):
        energy_ref[y] = wide[y * owned : (y + 1) * owned, :].T[0:8, :]


def project_kernel(gradient_ref, unit_ref, scale_ref, inner_ref, share_hbm, share, sems):
    count, owned, width = share.shape
    domains = unit_ref.shape[0] // owned
    blocks = count // domains
    scale = scale_ref[...] * (1.0 / LIFT)
    sends = []
    for i in range(0, blocks, RUN):
        for p in range(i, i + RUN):
            lanes = slice(p * width, (p + 1) * width)
            part = (
                gradient_ref[:, lanes] * scale - unit_ref[:, lanes].astype(F32) * inner_ref[...]
            ).astype(BF16)
            for y in range(domains):
                share[i * domains + y * RUN + p - i] = part[y * owned : (y + 1) * owned]
        for y in range(domains):
            at = pl.ds(i * domains + y * RUN, RUN)
            sends.append(pltpu.make_async_copy(share.at[at], share_hbm.at[at], sems.at[len(sends)]))
            sends[-1].start()
    for send in sends:
        send.wait()


def tail_kernel(parts_ref, deriv_ref, table_ref, out_ref):
    count, atoms, width = parts_ref.shape
    sides = []
    for y in range(2):
        total = parts_ref[y * RUN].astype(F32)
        for i in range(1, count // 2):
            total += parts_ref[i // RUN * 2 * RUN + y * RUN + i % RUN].astype(F32)
        sides.append(total)
    total = sides[0] + pltpu.roll(sides[1], width // 2, 1)
    pairs = deriv_ref.shape[1]
    high = total.astype(BF16)
    low = (total - high.astype(F32)).astype(BF16)
    both = jnp.concatenate([high, low], axis=0)
    row = lax.broadcasted_iota(jnp.int32, (atoms, pairs), 0)
    lane = lax.broadcasted_iota(jnp.int32, (atoms, pairs), 1)
    diagonal = row == lane % atoms
    rows = []
    for c in range(3):
        f = lax.dot_general(both, deriv_ref[c], LAST, preferred_element_type=F32)
        f = jnp.where(diagonal, f[:atoms] + f[atoms:], 0.0)
        rows.append(jnp.sum(f, axis=0, keepdims=True))
    partial = jnp.concatenate(rows + [jnp.zeros((5, pairs), F32)], axis=0)
    first = partial.astype(BF16)
    rest = partial - first.astype(F32)
    second = rest.astype(BF16)
    third = (rest - second.astype(F32)).astype(BF16)
    pieces = jnp.concatenate([first.astype(F32), second.astype(F32), third.astype(F32)], axis=0)
    moved = jnp.dot(pieces.astype(BF16), table_ref[...], preferred_element_type=F32)
    out_ref[...] = moved[0:8] + moved[8:16] + moved[16:24]


def body(descriptors, sparse_points, coefficients, derivatives, neighbours, counts, ghost_index):
    yl = lax.axis_index("yl")
    first = yl == 0
    owned, width = descriptors.shape
    points, part = sparse_points.shape
    n_sp, n_plane = lax.axis_size(SP), lax.axis_size(PLANE)
    columns = n_sp * width
    half = points // 2
    atoms = 2 * owned
    slots_count = neighbours.shape[1]
    pairs_count = owned * slots_count
    ghosts = ghost_index.shape[0] // 2
    swap = [(0, 1), (1, 0)]
    vmem = pl.BlockSpec(memory_space=pltpu.VMEM)
    smem = pl.BlockSpec(memory_space=pltpu.SMEM)
    anywhere = pl.BlockSpec(memory_space=pl.ANY)

    side = yl.reshape(1).astype(jnp.int32)

    with jax.named_scope("points_swap"):
        turned = sparse_points.T
        kept = lax.dynamic_slice_in_dim(turned, yl * half, half, 1).astype(F32) * LIFT
        sent = lax.dynamic_slice_in_dim(turned, (1 - yl) * half, half, 1).astype(F32) * LIFT
        got = lax.ppermute(sent.astype(F16), "yl", swap)
        block = jnp.concatenate([kept.astype(F16), got], axis=0)
    with jax.named_scope("points_gather"):
        lifted = lax.all_gather(block, "z", axis=0, tiled=True)

    with jax.named_scope("descriptors_gather"):
        spread = pl.pallas_call(
            spread_kernel,
            out_shape=jax.ShapeDtypeStruct((n_plane, owned, width), BF16),
            in_specs=[anywhere],
            out_specs=anywhere,
            scratch_shapes=[pltpu.SemaphoreType.DMA((n_plane,))],
            compiler_params=pltpu.CompilerParams(vmem_limit_bytes=4 << 20),
        )(descriptors)
        rows = lax.all_to_all(spread, PLANE, 0, 0)
        unit_rows, scale = pl.pallas_call(
            prepare_kernel,
            out_shape=(
                jax.ShapeDtypeStruct((atoms, columns), BF16),
                jax.ShapeDtypeStruct((atoms, width), F32),
            ),
            in_specs=[smem, vmem],
            out_specs=(vmem, vmem),
            compiler_params=pltpu.CompilerParams(vmem_limit_bytes=16 << 20),
            cost_estimate=pl.CostEstimate(
                flops=8 * atoms * columns, bytes_accessed=4 << 20, transcendentals=0
            ),
        )(side, rows)

    with jax.named_scope("kernel"):
        kernel = jnp.dot(unit_rows, lifted.astype(BF16), preferred_element_type=F32)
        slopes, inner, energy_part = pl.pallas_call(
            slope_kernel,
            out_shape=(
                jax.ShapeDtypeStruct((atoms, half), BF16),
                jax.ShapeDtypeStruct((atoms, width), F32),
                jax.ShapeDtypeStruct((2, 8, owned), F32),
            ),
            in_specs=[smem] + [vmem] * 3,
            out_specs=(vmem, vmem, vmem),
            scratch_shapes=[pltpu.VMEM((atoms, width), F32)],
            compiler_params=pltpu.CompilerParams(vmem_limit_bytes=8 << 20),
        )(side, kernel, scale, coefficients.reshape(2, half))
    with jax.named_scope("gradient"):
        slopes, again = lax.optimization_barrier((slopes, lifted))
        gradient = lax.dot_general(
            slopes, again.astype(BF16), LAST, preferred_element_type=F32
        )
        outgoing = pl.pallas_call(
            project_kernel,
            out_shape=jax.ShapeDtypeStruct((n_plane, owned, width), BF16),
            in_specs=[vmem] * 4,
            out_specs=anywhere,
            scratch_shapes=[
                pltpu.VMEM((n_plane, owned, width), BF16),
                pltpu.SemaphoreType.DMA((8,)),
            ],
            compiler_params=pltpu.CompilerParams(vmem_limit_bytes=8 << 20),
        )(gradient, unit_rows, scale, inner)
    with jax.named_scope("gradient_exchange"):
        parts = lax.all_to_all(outgoing, PLANE, 0, 0)

    with jax.named_scope("scatter_table"):
        neighbours, counts, ghost_index, energy_part = lax.optimization_barrier(
            (neighbours, counts, ghost_index, energy_part)
        )
        slot_total = owned + 2 * ghosts
        flat = neighbours.T.reshape(pairs_count)
        slot_ids = jnp.arange(slot_total, dtype=jnp.int32)
        hot = (flat[:, None] == slot_ids[None, :]).astype(BF16)
        target = jnp.concatenate(
            [
                jnp.arange(owned, dtype=jnp.int32),
                ghost_index[:ghosts] + owned,
                ghost_index[ghosts:] + 2 * owned,
            ]
        )
        column_ids = jnp.arange(3 * owned, dtype=jnp.int32)
        moves = (target[:, None] == column_ids[None, :]).astype(BF16)
        landed = jnp.dot(hot, moves, preferred_element_type=F32)
        atom_of = jnp.arange(pairs_count, dtype=jnp.int32) % owned
        slot_of = jnp.arange(pairs_count, dtype=jnp.int32) // owned
        self_hot = (atom_of[:, None] == column_ids[None, :]).astype(F32)
        live = slot_of < jnp.tile(counts, slots_count)
        table = jnp.where(live[:, None], self_hot - landed, 0.0).astype(BF16)
        lined = jnp.transpose(derivatives, (1, 2, 0, 3)).reshape(3, pairs_count, width)

    with jax.named_scope("tail"):
        moved = pl.pallas_call(
            tail_kernel,
            out_shape=jax.ShapeDtypeStruct((8, 3 * owned), F32),
            in_specs=[vmem, vmem, vmem],
            out_specs=vmem,
            compiler_params=pltpu.CompilerParams(vmem_limit_bytes=24 << 20),
            cost_estimate=pl.CostEstimate(
                flops=12 * owned * width * pairs_count, bytes_accessed=4 << 20, transcendentals=0
            ),
        )(parts, lined, table)
        keep, to_left, to_right = jnp.split(moved[:3], 3, axis=1)
    with jax.named_scope("ghosts"):
        across = jnp.where(first, to_left, to_right)
        beside = jnp.where(first, to_right, to_left)
        size = lax.axis_size(DOM)
        pairs = [(i, (i - 1) % size if i % 2 == 0 else (i + 1) % size) for i in range(size)]
        keep = keep + lax.ppermute(across, DOM, pairs)
        both = jnp.stack([jnp.where(first, keep, beside), jnp.where(first, beside, keep)])
        both = jnp.concatenate([both, energy_part[:, :1]], axis=1)
        both = jnp.broadcast_to(both[None, :, None], (n_sp // RUN, 2, RUN, 4, owned))
        both = both.reshape(n_plane, 4, owned)
        received = jnp.sum(lax.all_to_all(both, PLANE, 0, 0), axis=0)
    return (received[:3], received[3])


def solution(mesh):
    grid = Mesh(mesh.devices.reshape(16, 2, 4, 2, 2), ("z", "yl", "x", "yh", "c"))
    return jax.shard_map(
        body,
        mesh=grid,
        in_specs=(
            P(DOM, SP),
            P(SP, DOM),
            P(SP),
            P(DOM, None, None, SP),
            P(DOM, None),
            P(DOM),
            P(DOM),
        ),
        out_specs=(P(None, DOM), P(DOM)),
        check_vma=False,
    )
```

```python
import jax
import jax.numpy as jnp
from jax import lax
from jax.experimental import pallas as pl
from jax.experimental.pallas import tpu as pltpu
from jax.sharding import Mesh, PartitionSpec as P

DOM = ("z", "yl")
SP = ("x", "yh", "c")
CHIPS = ("x", "yl", "yh")
HALF = 2
RUN = 4
PLANE = ("x", "yl", "yh", "c")
LIFT = 8192.0
F32, BF16, F16 = jnp.float32, jnp.bfloat16, jnp.float16
LAST = (((1,), (1,)), ((), ()))


def spread_kernel(rows_ref, out_hbm, sems):
    copies = [
        pltpu.make_async_copy(rows_ref, out_hbm.at[i], sems.at[i]) for i in range(out_hbm.shape[0])
    ]
    for copy in copies:
        copy.start()
    for copy in copies:
        copy.wait()


def prepare_kernel(side_ref, rows_ref, unit_ref, scale_ref):
    domains = 2
    blocks = rows_ref.shape[0] // domains
    owned, width = rows_ref.shape[1:]
    at = [[s // RUN * 2 * RUN + y * RUN + s % RUN for s in range(blocks)] for y in range(domains)]
    shift = side_ref[0] * (width // 2)
    for y in range(domains):
        total = jnp.zeros((owned, width), F32)
        for s in range(blocks):
            value = rows_ref[at[y][s]].astype(F32)
            total += value * value
        norm = jnp.sqrt(jnp.sum(total, axis=1, keepdims=True) + 1e-06)
        scale = jnp.broadcast_to(1.0 / norm, (owned, width))
        scale_ref[y * owned : (y + 1) * owned, :] = scale
        for s in range(blocks):
            value = rows_ref[at[y][s]].astype(F32) * (scale * (1.0 / LIFT))
            unit_ref[y * owned : (y + 1) * owned, s * width : (s + 1) * width] = pltpu.roll(
                value, shift, 1
            ).astype(BF16)


def slope_kernel(side_ref, kernel_ref, scale_ref, coef_ref, slopes_ref, inner_ref, energy_ref, wide):
    atoms = kernel_ref.shape[0]
    domains = energy_ref.shape[0]
    owned = atoms // domains
    four = 4.0 * coef_ref[pl.ds(side_ref[0], 1), :]
    rows = 32
    for r in range(0, atoms, rows):
        k = kernel_ref[r : r + rows, :]
        s = four * (k * k * k)
        low = s.astype(BF16)
        slopes_ref[r : r + rows, :] = low
        inner_ref[r : r + rows, :] = (scale_ref[r : r + rows, :] * LIFT) * jnp.sum(
            low.astype(F32) * k, axis=1, keepdims=True
        )
        wide[r : r + rows, :] = jnp.broadcast_to(
            0.25 * jnp.sum(s * k, axis=1, keepdims=True), (rows, 128)
        )
    for y in range(domains):
        energy_ref[y] = wide[y * owned : (y + 1) * owned, :].T[0:8, :]


def project_kernel(core_ref, gradient_ref, unit_ref, scale_ref, inner_ref, own_ref, other_ref):
    count, owned, width = own_ref.shape
    domains = unit_ref.shape[0] // owned
    scale = scale_ref[...] * (1.0 / LIFT)
    for j in range(count // domains):
        for ref, core in ((own_ref, core_ref[0]), (other_ref, 1 - core_ref[0])):
            lanes = pl.ds(pl.multiple_of((2 * j + core) * width, width), width)
            part = gradient_ref[:, lanes] * scale - unit_ref[:, lanes].astype(F32) * inner_ref[...]
            for y in range(domains):
                at = j // HALF * 2 * HALF + y * HALF + j % HALF
                ref[at] = part[y * owned : (y + 1) * owned].astype(ref.dtype)


def tail_kernel(parts_ref, deriv_ref, table_ref, out_ref):
    count, atoms, width = parts_ref.shape
    sides = []
    for y in range(2):
        total = parts_ref[y * HALF].astype(F32)
        for i in range(1, count // 2):
            total += parts_ref[i // HALF * 2 * HALF + y * HALF + i % HALF].astype(F32)
        sides.append(total)
    total = sides[0] + pltpu.roll(sides[1], width // 2, 1)
    pairs = deriv_ref.shape[1]
    high = total.astype(BF16)
    low = (total - high.astype(F32)).astype(BF16)
    both = jnp.concatenate([high, low], axis=0)
    row = lax.broadcasted_iota(jnp.int32, (atoms, pairs), 0)
    lane = lax.broadcasted_iota(jnp.int32, (atoms, pairs), 1)
    diagonal = row == lane % atoms
    rows = []
    for c in range(3):
        f = lax.dot_general(both, deriv_ref[c], LAST, preferred_element_type=F32)
        f = jnp.where(diagonal, f[:atoms] + f[atoms:], 0.0)
        rows.append(jnp.sum(f, axis=0, keepdims=True))
    partial = jnp.concatenate(rows + [jnp.zeros((5, pairs), F32)], axis=0)
    first = partial.astype(BF16)
    rest = partial - first.astype(F32)
    second = rest.astype(BF16)
    third = (rest - second.astype(F32)).astype(BF16)
    pieces = jnp.concatenate([first.astype(F32), second.astype(F32), third.astype(F32)], axis=0)
    moved = jnp.dot(pieces.astype(BF16), table_ref[...], preferred_element_type=F32)
    out_ref[...] = moved[0:8] + moved[8:16] + moved[16:24]


def body(descriptors, sparse_points, coefficients, derivatives, neighbours, counts, ghost_index):
    yl = lax.axis_index("yl")
    first = yl == 0
    owned, width = descriptors.shape
    points, part = sparse_points.shape
    n_sp, n_plane = lax.axis_size(SP), lax.axis_size(PLANE)
    columns = n_sp * width
    half = points // 2
    atoms = 2 * owned
    slots_count = neighbours.shape[1]
    pairs_count = owned * slots_count
    ghosts = ghost_index.shape[0] // 2
    swap = [(0, 1), (1, 0)]
    vmem = pl.BlockSpec(memory_space=pltpu.VMEM)
    smem = pl.BlockSpec(memory_space=pltpu.SMEM)
    anywhere = pl.BlockSpec(memory_space=pl.ANY)

    side = yl.reshape(1).astype(jnp.int32)
    core = lax.axis_index("c").reshape(1).astype(jnp.int32)

    with jax.named_scope("points_swap"):
        turned = sparse_points.T
        kept = lax.dynamic_slice_in_dim(turned, yl * half, half, 1).astype(F32) * LIFT
        sent = lax.dynamic_slice_in_dim(turned, (1 - yl) * half, half, 1).astype(F32) * LIFT
        got = lax.ppermute(sent.astype(F16), "yl", swap)
        block = jnp.concatenate([kept.astype(F16), got], axis=0)
    with jax.named_scope("points_gather"):
        lifted = lax.all_gather(block, "z", axis=0, tiled=True)

    with jax.named_scope("descriptors_gather"):
        spread = pl.pallas_call(
            spread_kernel,
            out_shape=jax.ShapeDtypeStruct((n_plane, owned, width), BF16),
            in_specs=[anywhere],
            out_specs=anywhere,
            scratch_shapes=[pltpu.SemaphoreType.DMA((n_plane,))],
            compiler_params=pltpu.CompilerParams(vmem_limit_bytes=4 << 20),
        )(descriptors)
        rows = lax.all_to_all(spread, PLANE, 0, 0)
        unit_rows, scale = pl.pallas_call(
            prepare_kernel,
            out_shape=(
                jax.ShapeDtypeStruct((atoms, columns), BF16),
                jax.ShapeDtypeStruct((atoms, width), F32),
            ),
            in_specs=[smem, vmem],
            out_specs=(vmem, vmem),
            compiler_params=pltpu.CompilerParams(vmem_limit_bytes=16 << 20),
            cost_estimate=pl.CostEstimate(
                flops=8 * atoms * columns, bytes_accessed=4 << 20, transcendentals=0
            ),
        )(side, rows)

    with jax.named_scope("kernel"):
        kernel = jnp.dot(unit_rows, lifted.astype(BF16), preferred_element_type=F32)
        slopes, inner, energy_part = pl.pallas_call(
            slope_kernel,
            out_shape=(
                jax.ShapeDtypeStruct((atoms, half), BF16),
                jax.ShapeDtypeStruct((atoms, width), F32),
                jax.ShapeDtypeStruct((2, 8, owned), F32),
            ),
            in_specs=[smem] + [vmem] * 3,
            out_specs=(vmem, vmem, vmem),
            scratch_shapes=[pltpu.VMEM((atoms, width), F32)],
            compiler_params=pltpu.CompilerParams(vmem_limit_bytes=8 << 20),
        )(side, kernel, scale, coefficients.reshape(2, half))
    with jax.named_scope("gradient"):
        slopes, again = lax.optimization_barrier((slopes, lifted))
        gradient = lax.dot_general(
            slopes, again.astype(BF16), LAST, preferred_element_type=F32
        )
        own, other = pl.pallas_call(
            project_kernel,
            out_shape=(
                jax.ShapeDtypeStruct((n_plane // 2, owned, width), F32),
                jax.ShapeDtypeStruct((n_plane // 2, owned, width), BF16),
            ),
            in_specs=[smem] + [vmem] * 4,
            out_specs=(vmem, vmem),
            compiler_params=pltpu.CompilerParams(vmem_limit_bytes=12 << 20),
        )(core, gradient, unit_rows, scale, inner)
    with jax.named_scope("core_pair"):
        theirs = lax.ppermute(other, "c", swap)
        outgoing = (own + theirs.astype(F32)).astype(BF16)
    with jax.named_scope("gradient_exchange"):
        parts = lax.all_to_all(outgoing, CHIPS, 0, 0)

    with jax.named_scope("scatter_table"):
        neighbours, counts, ghost_index, energy_part = lax.optimization_barrier(
            (neighbours, counts, ghost_index, energy_part)
        )
        slot_total = owned + 2 * ghosts
        flat = neighbours.T.reshape(pairs_count)
        slot_ids = jnp.arange(slot_total, dtype=jnp.int32)
        hot = (flat[:, None] == slot_ids[None, :]).astype(BF16)
        target = jnp.concatenate(
            [
                jnp.arange(owned, dtype=jnp.int32),
                ghost_index[:ghosts] + owned,
                ghost_index[ghosts:] + 2 * owned,
            ]
        )
        column_ids = jnp.arange(3 * owned, dtype=jnp.int32)
        moves = (target[:, None] == column_ids[None, :]).astype(BF16)
        landed = jnp.dot(hot, moves, preferred_element_type=F32)
        atom_of = jnp.arange(pairs_count, dtype=jnp.int32) % owned
        slot_of = jnp.arange(pairs_count, dtype=jnp.int32) // owned
        self_hot = (atom_of[:, None] == column_ids[None, :]).astype(F32)
        live = slot_of < jnp.tile(counts, slots_count)
        table = jnp.where(live[:, None], self_hot - landed, 0.0).astype(BF16)
        lined = jnp.transpose(derivatives, (1, 2, 0, 3)).reshape(3, pairs_count, width)

    with jax.named_scope("tail"):
        moved = pl.pallas_call(
            tail_kernel,
            out_shape=jax.ShapeDtypeStruct((8, 3 * owned), F32),
            in_specs=[vmem, vmem, vmem],
            out_specs=vmem,
            compiler_params=pltpu.CompilerParams(vmem_limit_bytes=24 << 20),
            cost_estimate=pl.CostEstimate(
                flops=12 * owned * width * pairs_count, bytes_accessed=4 << 20, transcendentals=0
            ),
        )(parts, lined, table)
        keep, to_left, to_right = jnp.split(moved[:3], 3, axis=1)
    with jax.named_scope("ghosts"):
        across = jnp.where(first, to_left, to_right)
        beside = jnp.where(first, to_right, to_left)
        size = lax.axis_size(DOM)
        pairs = [(i, (i - 1) % size if i % 2 == 0 else (i + 1) % size) for i in range(size)]
        keep = keep + lax.ppermute(across, DOM, pairs)
        both = jnp.stack([jnp.where(first, keep, beside), jnp.where(first, beside, keep)])
        both = jnp.concatenate([both, energy_part[:, :1]], axis=1)
        both = jnp.broadcast_to(both[None, :, None], (n_sp // RUN, 2, RUN, 4, owned))
        both = both.reshape(n_plane, 4, owned)
        received = jnp.sum(lax.all_to_all(both, PLANE, 0, 0), axis=0)
    return (received[:3], received[3])


def solution(mesh):
    grid = Mesh(mesh.devices.reshape(16, 2, 4, 2, 2), ("z", "yl", "x", "yh", "c"))
    return jax.shard_map(
        body,
        mesh=grid,
        in_specs=(
            P(DOM, SP),
            P(SP, DOM),
            P(SP),
            P(DOM, None, None, SP),
            P(DOM, None),
            P(DOM),
            P(DOM),
        ),
        out_specs=(P(None, DOM), P(DOM)),
        check_vma=False,
    )
```

```python
import jax
import jax.numpy as jnp
from jax import lax
from jax.experimental import pallas as pl
from jax.experimental.pallas import tpu as pltpu
from jax.sharding import Mesh, PartitionSpec as P

DOM = ("z", "yl")
SP = ("x", "yh", "c")
CHIPS = ("x", "yl", "yh")
HALF = 2
RUN = 4
PLANE = ("x", "yl", "yh", "c")
LIFT = 8192.0
F32, BF16, F16 = jnp.float32, jnp.bfloat16, jnp.float16
LAST = (((1,), (1,)), ((), ()))


def spread_kernel(rows_ref, out_hbm, few, sems):
    count = few.shape[0]
    for i in range(count):
        few[i] = rows_ref[...]
    copies = [
        pltpu.make_async_copy(few, out_hbm.at[pl.ds(i * count, count)], sems.at[i])
        for i in range(out_hbm.shape[0] // count)
    ]
    for copy in copies:
        copy.start()
    for copy in copies:
        copy.wait()


def prepare_kernel(side_ref, rows_ref, unit_ref, scale_ref):
    domains = 2
    blocks = rows_ref.shape[0] // domains
    owned, width = rows_ref.shape[1:]
    at = [[s // RUN * 2 * RUN + y * RUN + s % RUN for s in range(blocks)] for y in range(domains)]
    shift = side_ref[0] * (width // 2)
    for y in range(domains):
        total = jnp.zeros((owned, width), F32)
        for s in range(blocks):
            value = rows_ref[at[y][s]].astype(F32)
            total += value * value
        norm = jnp.sqrt(jnp.sum(total, axis=1, keepdims=True) + 1e-06)
        scale = jnp.broadcast_to(1.0 / norm, (owned, width))
        scale_ref[y * owned : (y + 1) * owned, :] = scale
        for s in range(blocks):
            value = rows_ref[at[y][s]].astype(F32) * (scale * (1.0 / LIFT))
            unit_ref[y * owned : (y + 1) * owned, s * width : (s + 1) * width] = pltpu.roll(
                value, shift, 1
            ).astype(BF16)


def slope_kernel(side_ref, kernel_ref, scale_ref, coef_ref, slopes_ref, inner_ref, energy_ref, wide):
    atoms = kernel_ref.shape[0]
    domains = energy_ref.shape[0]
    owned = atoms // domains
    four = 4.0 * coef_ref[pl.ds(side_ref[0], 1), :]
    rows = 32
    for r in range(0, atoms, rows):
        k = kernel_ref[r : r + rows, :]
        s = four * (k * k * k)
        low = s.astype(BF16)
        slopes_ref[r : r + rows, :] = low
        inner_ref[r : r + rows, :] = (scale_ref[r : r + rows, :] * LIFT) * jnp.sum(
            low.astype(F32) * k, axis=1, keepdims=True
        )
        wide[r : r + rows, :] = jnp.broadcast_to(
            0.25 * jnp.sum(s * k, axis=1, keepdims=True), (rows, 128)
        )
    for y in range(domains):
        energy_ref[y] = wide[y * owned : (y + 1) * owned, :].T[0:8, :]


def project_kernel(core_ref, gradient_ref, unit_ref, scale_ref, inner_ref, own_ref, other_ref):
    count, owned, width = own_ref.shape
    domains = unit_ref.shape[0] // owned
    scale = scale_ref[...] * (1.0 / LIFT)
    for j in range(count // domains):
        for ref, core in ((own_ref, core_ref[0]), (other_ref, 1 - core_ref[0])):
            lanes = pl.ds(pl.multiple_of((2 * j + core) * width, width), width)
            part = gradient_ref[:, lanes] * scale - unit_ref[:, lanes].astype(F32) * inner_ref[...]
            for y in range(domains):
                at = j // HALF * 2 * HALF + y * HALF + j % HALF
                ref[at] = part[y * owned : (y + 1) * owned].astype(ref.dtype)


def tail_kernel(parts_ref, deriv_ref, table_ref, out_ref):
    count, atoms, width = parts_ref.shape
    sides = []
    for y in range(2):
        total = parts_ref[y * HALF].astype(F32)
        for i in range(1, count // 2):
            total += parts_ref[i // HALF * 2 * HALF + y * HALF + i % HALF].astype(F32)
        sides.append(total)
    total = sides[0] + pltpu.roll(sides[1], width // 2, 1)
    pairs = deriv_ref.shape[1]
    high = total.astype(BF16)
    low = (total - high.astype(F32)).astype(BF16)
    both = jnp.concatenate([high, low], axis=0)
    row = lax.broadcasted_iota(jnp.int32, (atoms, pairs), 0)
    lane = lax.broadcasted_iota(jnp.int32, (atoms, pairs), 1)
    diagonal = row == lane % atoms
    rows = []
    for c in range(3):
        f = lax.dot_general(both, deriv_ref[c], LAST, preferred_element_type=F32)
        f = jnp.where(diagonal, f[:atoms] + f[atoms:], 0.0)
        rows.append(jnp.sum(f, axis=0, keepdims=True))
    partial = jnp.concatenate(rows + [jnp.zeros((5, pairs), F32)], axis=0)
    first = partial.astype(BF16)
    rest = partial - first.astype(F32)
    second = rest.astype(BF16)
    third = (rest - second.astype(F32)).astype(BF16)
    pieces = jnp.concatenate([first.astype(F32), second.astype(F32), third.astype(F32)], axis=0)
    moved = jnp.dot(pieces.astype(BF16), table_ref[...], preferred_element_type=F32)
    out_ref[...] = moved[0:8] + moved[8:16] + moved[16:24]


def body(descriptors, sparse_points, coefficients, derivatives, neighbours, counts, ghost_index):
    yl = lax.axis_index("yl")
    first = yl == 0
    owned, width = descriptors.shape
    points, part = sparse_points.shape
    n_sp, n_plane = lax.axis_size(SP), lax.axis_size(PLANE)
    columns = n_sp * width
    half = points // 2
    atoms = 2 * owned
    slots_count = neighbours.shape[1]
    pairs_count = owned * slots_count
    ghosts = ghost_index.shape[0] // 2
    swap = [(0, 1), (1, 0)]
    vmem = pl.BlockSpec(memory_space=pltpu.VMEM)
    smem = pl.BlockSpec(memory_space=pltpu.SMEM)
    anywhere = pl.BlockSpec(memory_space=pl.ANY)

    side = yl.reshape(1).astype(jnp.int32)
    core = lax.axis_index("c").reshape(1).astype(jnp.int32)

    with jax.named_scope("points_swap"):
        turned = sparse_points.T
        kept = lax.dynamic_slice_in_dim(turned, yl * half, half, 1).astype(F32) * LIFT
        sent = lax.dynamic_slice_in_dim(turned, (1 - yl) * half, half, 1).astype(F32) * LIFT
        got = lax.ppermute(sent.astype(F16), "yl", swap)
        block = jnp.concatenate([kept.astype(F16), got], axis=0)
    with jax.named_scope("points_gather"):
        lifted = lax.all_gather(block, "z", axis=0, tiled=True)

    with jax.named_scope("descriptors_gather"):
        spread = pl.pallas_call(
            spread_kernel,
            out_shape=jax.ShapeDtypeStruct((n_plane, owned, width), BF16),
            in_specs=[vmem],
            out_specs=anywhere,
            scratch_shapes=[
                pltpu.VMEM((4, owned, width), BF16),
                pltpu.SemaphoreType.DMA((n_plane // 4,)),
            ],
            compiler_params=pltpu.CompilerParams(vmem_limit_bytes=4 << 20),
        )(descriptors)
        rows = lax.all_to_all(spread, PLANE, 0, 0)
        unit_rows, scale = pl.pallas_call(
            prepare_kernel,
            out_shape=(
                jax.ShapeDtypeStruct((atoms, columns), BF16),
                jax.ShapeDtypeStruct((atoms, width), F32),
            ),
            in_specs=[smem, vmem],
            out_specs=(vmem, vmem),
            compiler_params=pltpu.CompilerParams(vmem_limit_bytes=16 << 20),
            cost_estimate=pl.CostEstimate(
                flops=8 * atoms * columns, bytes_accessed=4 << 20, transcendentals=0
            ),
        )(side, rows)

    with jax.named_scope("kernel"):
        kernel = jnp.dot(unit_rows, lifted.astype(BF16), preferred_element_type=F32)
        slopes, inner, energy_part = pl.pallas_call(
            slope_kernel,
            out_shape=(
                jax.ShapeDtypeStruct((atoms, half), BF16),
                jax.ShapeDtypeStruct((atoms, width), F32),
                jax.ShapeDtypeStruct((2, 8, owned), F32),
            ),
            in_specs=[smem] + [vmem] * 3,
            out_specs=(vmem, vmem, vmem),
            scratch_shapes=[pltpu.VMEM((atoms, width), F32)],
            compiler_params=pltpu.CompilerParams(vmem_limit_bytes=8 << 20),
        )(side, kernel, scale, coefficients.reshape(2, half))
    with jax.named_scope("gradient"):
        slopes, again = lax.optimization_barrier((slopes, lifted))
        gradient = lax.dot_general(
            slopes, again.astype(BF16), LAST, preferred_element_type=F32
        )
        own, other = pl.pallas_call(
            project_kernel,
            out_shape=(
                jax.ShapeDtypeStruct((n_plane // 2, owned, width), F32),
                jax.ShapeDtypeStruct((n_plane // 2, owned, width), BF16),
            ),
            in_specs=[smem] + [vmem] * 4,
            out_specs=(vmem, vmem),
            compiler_params=pltpu.CompilerParams(vmem_limit_bytes=12 << 20),
        )(core, gradient, unit_rows, scale, inner)
    with jax.named_scope("core_pair"):
        theirs = lax.ppermute(other, "c", swap)
        outgoing = (own + theirs.astype(F32)).astype(BF16)
    with jax.named_scope("gradient_exchange"):
        parts = lax.all_to_all(outgoing, CHIPS, 0, 0)

    with jax.named_scope("scatter_table"):
        neighbours, counts, ghost_index, energy_part = lax.optimization_barrier(
            (neighbours, counts, ghost_index, energy_part)
        )
        slot_total = owned + 2 * ghosts
        flat = neighbours.T.reshape(pairs_count)
        slot_ids = jnp.arange(slot_total, dtype=jnp.int32)
        hot = (flat[:, None] == slot_ids[None, :]).astype(BF16)
        target = jnp.concatenate(
            [
                jnp.arange(owned, dtype=jnp.int32),
                ghost_index[:ghosts] + owned,
                ghost_index[ghosts:] + 2 * owned,
            ]
        )
        column_ids = jnp.arange(3 * owned, dtype=jnp.int32)
        moves = (target[:, None] == column_ids[None, :]).astype(BF16)
        landed = jnp.dot(hot, moves, preferred_element_type=F32)
        atom_of = jnp.arange(pairs_count, dtype=jnp.int32) % owned
        slot_of = jnp.arange(pairs_count, dtype=jnp.int32) // owned
        self_hot = (atom_of[:, None] == column_ids[None, :]).astype(F32)
        live = slot_of < jnp.tile(counts, slots_count)
        table = jnp.where(live[:, None], self_hot - landed, 0.0).astype(BF16)
        lined = jnp.transpose(derivatives, (1, 2, 0, 3)).reshape(3, pairs_count, width)

    with jax.named_scope("tail"):
        moved = pl.pallas_call(
            tail_kernel,
            out_shape=jax.ShapeDtypeStruct((8, 3 * owned), F32),
            in_specs=[vmem, vmem, vmem],
            out_specs=vmem,
            compiler_params=pltpu.CompilerParams(vmem_limit_bytes=24 << 20),
            cost_estimate=pl.CostEstimate(
                flops=12 * owned * width * pairs_count, bytes_accessed=4 << 20, transcendentals=0
            ),
        )(parts, lined, table)
        keep, to_left, to_right = jnp.split(moved[:3], 3, axis=1)
    with jax.named_scope("ghosts"):
        across = jnp.where(first, to_left, to_right)
        beside = jnp.where(first, to_right, to_left)
        size = lax.axis_size(DOM)
        pairs = [(i, (i - 1) % size if i % 2 == 0 else (i + 1) % size) for i in range(size)]
        keep = keep + lax.ppermute(across, DOM, pairs)
        both = jnp.stack([jnp.where(first, keep, beside), jnp.where(first, beside, keep)])
        both = jnp.concatenate([both, energy_part[:, :1]], axis=1)
        both = jnp.broadcast_to(both[None, :, None], (n_sp // RUN, 2, RUN, 4, owned))
        both = both.reshape(n_plane, 4, owned)
        received = jnp.sum(lax.all_to_all(both, PLANE, 0, 0), axis=0)
    return (received[:3], received[3])


def solution(mesh):
    grid = Mesh(mesh.devices.reshape(16, 2, 4, 2, 2), ("z", "yl", "x", "yh", "c"))
    return jax.shard_map(
        body,
        mesh=grid,
        in_specs=(
            P(DOM, SP),
            P(SP, DOM),
            P(SP),
            P(DOM, None, None, SP),
            P(DOM, None),
            P(DOM),
            P(DOM),
        ),
        out_specs=(P(None, DOM), P(DOM)),
        check_vma=False,
    )
```

```python
import jax
import jax.numpy as jnp
from jax import lax
from jax.experimental import pallas as pl
from jax.experimental.pallas import tpu as pltpu
from jax.sharding import Mesh, PartitionSpec as P

DOM = ("z", "yl")
SP = ("x", "yh", "c")
CHIPS = ("x", "yl", "yh")
HALF = 2
RUN = 4
PLANE = ("x", "yl", "yh", "c")
LIFT = 8192.0
F32, BF16, F16 = jnp.float32, jnp.bfloat16, jnp.float16
LAST = (((1,), (1,)), ((), ()))


def spread_kernel(rows_ref, out_hbm, few, sems):
    count = few.shape[0]
    for i in range(count):
        few[i] = rows_ref[...]
    copies = [
        pltpu.make_async_copy(few, out_hbm.at[pl.ds(i * count, count)], sems.at[i])
        for i in range(out_hbm.shape[0] // count)
    ]
    for copy in copies:
        copy.start()
    for copy in copies:
        copy.wait()


def prepare_kernel(side_ref, rows_ref, unit_ref, scale_ref):
    domains = 2
    blocks = rows_ref.shape[0] // domains
    owned, width = rows_ref.shape[1:]
    at = [[s // RUN * 2 * RUN + y * RUN + s % RUN for s in range(blocks)] for y in range(domains)]
    shift = side_ref[0] * (width // 2)
    for y in range(domains):
        total = jnp.zeros((owned, width), F32)
        for s in range(blocks):
            value = rows_ref[at[y][s]].astype(F32)
            total += value * value
        norm = jnp.sqrt(jnp.sum(total, axis=1, keepdims=True) + 1e-06)
        scale = jnp.broadcast_to(1.0 / norm, (owned, width))
        scale_ref[y * owned : (y + 1) * owned, :] = scale
        for s in range(blocks):
            value = rows_ref[at[y][s]].astype(F32) * (scale * (1.0 / LIFT))
            unit_ref[y * owned : (y + 1) * owned, s * width : (s + 1) * width] = pltpu.roll(
                value, shift, 1
            ).astype(BF16)


def slope_kernel(side_ref, kernel_ref, scale_ref, coef_ref, slopes_ref, inner_ref, energy_ref, wide):
    atoms = kernel_ref.shape[0]
    domains = energy_ref.shape[0]
    owned = atoms // domains
    four = 4.0 * coef_ref[pl.ds(side_ref[0], 1), :]
    rows = 32
    for r in range(0, atoms, rows):
        k = kernel_ref[r : r + rows, :]
        s = four * (k * k * k)
        low = s.astype(BF16)
        slopes_ref[r : r + rows, :] = low
        inner_ref[r : r + rows, :] = (scale_ref[r : r + rows, :] * LIFT) * jnp.sum(
            low.astype(F32) * k, axis=1, keepdims=True
        )
        wide[r : r + rows, :] = jnp.broadcast_to(
            0.25 * jnp.sum(s * k, axis=1, keepdims=True), (rows, 128)
        )
    for y in range(domains):
        energy_ref[y] = wide[y * owned : (y + 1) * owned, :].T[0:8, :]


def project_kernel(core_ref, gradient_ref, unit_ref, scale_ref, inner_ref, own_ref, other_ref):
    count, owned, width = own_ref.shape
    domains = unit_ref.shape[0] // owned
    scale = scale_ref[...] * (1.0 / LIFT)
    for j in range(count // domains):
        for ref, core in ((own_ref, core_ref[0]), (other_ref, 1 - core_ref[0])):
            lanes = pl.ds(pl.multiple_of((2 * j + core) * width, width), width)
            part = gradient_ref[:, lanes] * scale - unit_ref[:, lanes].astype(F32) * inner_ref[...]
            for y in range(domains):
                at = j // HALF * 2 * HALF + y * HALF + j % HALF
                ref[at] = part[y * owned : (y + 1) * owned].astype(ref.dtype)


def tail_kernel(parts_ref, deriv_ref, table_ref, out_ref):
    count, atoms, width = parts_ref.shape
    sides = []
    for y in range(2):
        total = parts_ref[y * HALF].astype(F32)
        for i in range(1, count // 2):
            total += parts_ref[i // HALF * 2 * HALF + y * HALF + i % HALF].astype(F32)
        sides.append(total)
    total = sides[0] + pltpu.roll(sides[1], width // 2, 1)
    pairs = deriv_ref.shape[1]
    high = total.astype(BF16)
    low = (total - high.astype(F32)).astype(BF16)
    both = jnp.concatenate([high, low], axis=0)
    row = lax.broadcasted_iota(jnp.int32, (atoms, pairs), 0)
    lane = lax.broadcasted_iota(jnp.int32, (atoms, pairs), 1)
    diagonal = row == lane % atoms
    rows = []
    for c in range(3):
        f = lax.dot_general(both, deriv_ref[c], LAST, preferred_element_type=F32)
        f = jnp.where(diagonal, f[:atoms] + f[atoms:], 0.0)
        rows.append(jnp.sum(f, axis=0, keepdims=True))
    partial = jnp.concatenate(rows + [jnp.zeros((5, pairs), F32)], axis=0)
    first = partial.astype(BF16)
    rest = partial - first.astype(F32)
    second = rest.astype(BF16)
    third = (rest - second.astype(F32)).astype(BF16)
    pieces = jnp.concatenate([first.astype(F32), second.astype(F32), third.astype(F32)], axis=0)
    moved = jnp.dot(pieces.astype(BF16), table_ref[...], preferred_element_type=F32)
    out_ref[...] = moved[0:8] + moved[8:16] + moved[16:24]


def body(descriptors, sparse_points, coefficients, derivatives, neighbours, counts, ghost_index):
    yl = lax.axis_index("yl")
    first = yl == 0
    owned, width = descriptors.shape
    points, part = sparse_points.shape
    n_sp, n_plane = lax.axis_size(SP), lax.axis_size(PLANE)
    columns = n_sp * width
    half = points // 2
    atoms = 2 * owned
    slots_count = neighbours.shape[1]
    pairs_count = owned * slots_count
    ghosts = ghost_index.shape[0] // 2
    swap = [(0, 1), (1, 0)]
    vmem = pl.BlockSpec(memory_space=pltpu.VMEM)
    smem = pl.BlockSpec(memory_space=pltpu.SMEM)
    anywhere = pl.BlockSpec(memory_space=pl.ANY)

    side = yl.reshape(1).astype(jnp.int32)
    core = lax.axis_index("c").reshape(1).astype(jnp.int32)

    with jax.named_scope("points_swap"):
        turned = sparse_points.T
        kept = lax.dynamic_slice_in_dim(turned, yl * half, half, 1).astype(F32) * LIFT
        sent = lax.dynamic_slice_in_dim(turned, (1 - yl) * half, half, 1).astype(F32) * LIFT
        got = lax.ppermute(sent.astype(F16), "yl", swap)
        block = jnp.concatenate([kept.astype(F16), got], axis=0)
    with jax.named_scope("points_gather"):
        lifted = lax.all_gather(block, "z", axis=0, tiled=True)

    with jax.named_scope("descriptors_gather"):
        spread = pl.pallas_call(
            spread_kernel,
            out_shape=jax.ShapeDtypeStruct((n_plane, owned, width), BF16),
            in_specs=[vmem],
            out_specs=anywhere,
            scratch_shapes=[
                pltpu.VMEM((4, owned, width), BF16),
                pltpu.SemaphoreType.DMA((n_plane // 4,)),
            ],
            compiler_params=pltpu.CompilerParams(vmem_limit_bytes=4 << 20),
        )(descriptors)
        rows = lax.all_to_all(spread, PLANE, 0, 0)
        unit_rows, scale = pl.pallas_call(
            prepare_kernel,
            out_shape=(
                jax.ShapeDtypeStruct((atoms, columns), BF16),
                jax.ShapeDtypeStruct((atoms, width), F32),
            ),
            in_specs=[smem, vmem],
            out_specs=(vmem, vmem),
            compiler_params=pltpu.CompilerParams(vmem_limit_bytes=16 << 20),
            cost_estimate=pl.CostEstimate(
                flops=8 * atoms * columns, bytes_accessed=4 << 20, transcendentals=0
            ),
        )(side, rows)

    with jax.named_scope("kernel"):
        middle = columns // 2
        kernel = jnp.dot(
            unit_rows[:, :middle], lifted[:middle].astype(BF16), preferred_element_type=F32
        ) + jnp.dot(unit_rows[:, middle:], lifted[middle:].astype(BF16), preferred_element_type=F32)
        slopes, inner, energy_part = pl.pallas_call(
            slope_kernel,
            out_shape=(
                jax.ShapeDtypeStruct((atoms, half), BF16),
                jax.ShapeDtypeStruct((atoms, width), F32),
                jax.ShapeDtypeStruct((2, 8, owned), F32),
            ),
            in_specs=[smem] + [vmem] * 3,
            out_specs=(vmem, vmem, vmem),
            scratch_shapes=[pltpu.VMEM((atoms, width), F32)],
            compiler_params=pltpu.CompilerParams(vmem_limit_bytes=8 << 20),
        )(side, kernel, scale, coefficients.reshape(2, half))
    with jax.named_scope("gradient"):
        slopes, again = lax.optimization_barrier((slopes, lifted))
        gradient = lax.dot_general(
            slopes, again.astype(BF16), LAST, preferred_element_type=F32
        )
        own, other = pl.pallas_call(
            project_kernel,
            out_shape=(
                jax.ShapeDtypeStruct((n_plane // 2, owned, width), F32),
                jax.ShapeDtypeStruct((n_plane // 2, owned, width), BF16),
            ),
            in_specs=[smem] + [vmem] * 4,
            out_specs=(vmem, vmem),
            compiler_params=pltpu.CompilerParams(vmem_limit_bytes=12 << 20),
        )(core, gradient, unit_rows, scale, inner)
    with jax.named_scope("core_pair"):
        theirs = lax.ppermute(other, "c", swap)
        outgoing = (own + theirs.astype(F32)).astype(BF16)
    with jax.named_scope("gradient_exchange"):
        parts = lax.all_to_all(outgoing, CHIPS, 0, 0)

    with jax.named_scope("scatter_table"):
        neighbours, counts, ghost_index, energy_part = lax.optimization_barrier(
            (neighbours, counts, ghost_index, energy_part)
        )
        slot_total = owned + 2 * ghosts
        flat = neighbours.T.reshape(pairs_count)
        slot_ids = jnp.arange(slot_total, dtype=jnp.int32)
        hot = (flat[:, None] == slot_ids[None, :]).astype(BF16)
        target = jnp.concatenate(
            [
                jnp.arange(owned, dtype=jnp.int32),
                ghost_index[:ghosts] + owned,
                ghost_index[ghosts:] + 2 * owned,
            ]
        )
        column_ids = jnp.arange(3 * owned, dtype=jnp.int32)
        moves = (target[:, None] == column_ids[None, :]).astype(BF16)
        landed = jnp.dot(hot, moves, preferred_element_type=F32)
        atom_of = jnp.arange(pairs_count, dtype=jnp.int32) % owned
        slot_of = jnp.arange(pairs_count, dtype=jnp.int32) // owned
        self_hot = (atom_of[:, None] == column_ids[None, :]).astype(F32)
        live = slot_of < jnp.tile(counts, slots_count)
        table = jnp.where(live[:, None], self_hot - landed, 0.0).astype(BF16)
        lined = jnp.transpose(derivatives, (1, 2, 0, 3)).reshape(3, pairs_count, width)

    with jax.named_scope("tail"):
        moved = pl.pallas_call(
            tail_kernel,
            out_shape=jax.ShapeDtypeStruct((8, 3 * owned), F32),
            in_specs=[vmem, vmem, vmem],
            out_specs=vmem,
            compiler_params=pltpu.CompilerParams(vmem_limit_bytes=24 << 20),
            cost_estimate=pl.CostEstimate(
                flops=12 * owned * width * pairs_count, bytes_accessed=4 << 20, transcendentals=0
            ),
        )(parts, lined, table)
        keep, to_left, to_right = jnp.split(moved[:3], 3, axis=1)
    with jax.named_scope("ghosts"):
        across = jnp.where(first, to_left, to_right)
        beside = jnp.where(first, to_right, to_left)
        size = lax.axis_size(DOM)
        pairs = [(i, (i - 1) % size if i % 2 == 0 else (i + 1) % size) for i in range(size)]
        keep = keep + lax.ppermute(across, DOM, pairs)
        both = jnp.stack([jnp.where(first, keep, beside), jnp.where(first, beside, keep)])
        both = jnp.concatenate([both, energy_part[:, :1]], axis=1)
        both = jnp.broadcast_to(both[None, :, None], (n_sp // RUN, 2, RUN, 4, owned))
        both = both.reshape(n_plane, 4, owned)
        received = jnp.sum(lax.all_to_all(both, PLANE, 0, 0), axis=0)
    return (received[:3], received[3])


def solution(mesh):
    grid = Mesh(mesh.devices.reshape(16, 2, 4, 2, 2), ("z", "yl", "x", "yh", "c"))
    return jax.shard_map(
        body,
        mesh=grid,
        in_specs=(
            P(DOM, SP),
            P(SP, DOM),
            P(SP),
            P(DOM, None, None, SP),
            P(DOM, None),
            P(DOM),
            P(DOM),
        ),
        out_specs=(P(None, DOM), P(DOM)),
        check_vma=False,
    )
```
